512 devices in a mesh: replica: 32 (over x_hi, z, core), fsdp: 16 (over x_lo, y).
Axes of the slice: x: 4 (x_hi: 2, x_lo: 2; x = x_hi * 2 + x_lo), y: 8, z: 8, core: 2. Of those that a mesh axis runs over, the one named last changes fastest.
Arguments:
- layer_input: bfloat16 [122880, 3072], P(('replica', 'fsdp')), may hold values from -24 to 24
- cotangent: bfloat16 [122880, 512], P(('replica', 'fsdp')), may hold values from -6 to 6
- local_weight: bfloat16 [32, 3072, 512], P('replica', 'fsdp'), may hold values from -0.21875 to 0.21875
- first_moment: float32 [32, 3072, 512], P('replica', 'fsdp'), may hold values from -128 to 128
- second_moment: float32 [32, 3072, 512], P('replica', 'fsdp'), may hold values from 100 to 10000
- anchor: float32 [3072, 512], P('fsdp', 'replica'), may hold values from -0.109375 to 0.109375
- outer_momentum: float32 [3072, 512], P('fsdp', 'replica'), may hold values from -0.3125 to 0.3125
Outputs:
- input_grad: bfloat16 [122880, 3072], P(('replica', 'fsdp'))
- new_weight: bfloat16 [32, 3072, 512], P('replica', 'fsdp')
- new_first: float32 [32, 3072, 512], P('replica', 'fsdp')
- new_second: float32 [32, 3072, 512], P('replica', 'fsdp')
- new_anchor: float32 [3072, 512], P('fsdp', 'replica')
- new_momentum: float32 [3072, 512], P('fsdp', 'replica')
The draws below stay inside these ranges and needn't reach their ends.
All inputs are finite; a program needn't handle non-finite values.
Results may differ from the reference program's by a relative error of at most 0.012.
Values may be sent and summed in bfloat16 or wider, within the bound.
A program may use at most 64 MiB of HBM per device.

```python
import math
import jax
import jax.numpy as jnp
from jax import lax

D = 3072
KV = 512
TOK_DEV = 240
TOKENS = 122880
N_REPLICA = 32
N_FSDP = 16


def with_spikes(array, own_key, source, target, blocks, factor):
    def block_of(position):
        return (jnp.arange(array.shape[position]) // (array.shape[position] // blocks)).reshape((-1,) + (1,) * (array.ndim - 1 - position))

    near = jax.random.permutation(own_key, blocks)[block_of(target)]
    far = (block_of(target) + blocks // 2) % blocks
    return jnp.where((block_of(source) == near) | (block_of(source) == far), factor * array, array)


def level_of(rng, extent, split, least, top_value):
    def one(position, shards_of):
        heights = jax.random.uniform(jax.random.fold_in(jax.random.fold_in(rng, 6), position), (shards_of,), jnp.float32, least / len(split), top_value / len(split))
        return jnp.repeat(jnp.exp(heights), extent[position] // shards_of).reshape((-1,) + (1,) * (len(extent) - position - 1))

    gain = one(*split[0])
    for cut in split[1:]:
        gain = gain * one(*cut)
    return gain


def normal_values(stream_key, extent, scale, reach, shards=(), kind=jnp.bfloat16):
    gain = level_of(stream_key, extent, shards, -0.22, 0.18) if shards else 1.0
    array = jax.random.normal(stream_key, extent, jnp.float32) * scale * gain
    return jnp.minimum(jnp.maximum(array, -reach), reach).astype(kind)


def gaussian_with(own_key, extent, spread, limit, split, heavy, kind=jnp.bfloat16):
    array = spread * jax.random.normal(own_key, extent, jnp.float32)
    if split:
        array = array * level_of(own_key, extent, split, -0.22, 0.18)
    return jnp.clip(with_spikes(array, jax.random.fold_in(own_key, 3), *heavy), -limit, limit).astype(kind)


def setup_inputs(seed: int = 0) -> dict:
    streams_of = jax.random.split(jax.random.key(seed), 8)
    return {
        "layer_input": gaussian_with(streams_of[0], (TOKENS, D), 1.0, 24.0, ((0, 512),), (0, 1, 512, 6.0)),
        "cotangent": normal_values(streams_of[1], (TOKENS, KV), 1.0, 6.0, ((0, 512),)),
        "local_weight": gaussian_with(streams_of[2], (N_REPLICA, D, KV), D ** -0.5, 0.21875, ((0, 32), (1, 16)), (0, 2, 32, 2.75)),
        "first_moment": normal_values(streams_of[3], (N_REPLICA, D, KV), 20.0, 128.0, ((0, 32), (1, 16)), jnp.float32),
        "second_moment": jnp.clip(jnp.exp(math.log(10000.0) - 4.6051702 * jax.random.uniform(streams_of[4], (N_REPLICA, D, KV), jnp.float32) ** level_of(streams_of[4], (N_REPLICA, D, KV), ((0, 32), (1, 16)), -0.2, 0.2)), 100.0, 10000.0),
        "anchor": normal_values(streams_of[5], (D, KV), D ** -0.5, 0.109375, ((0, 16), (1, 32)), jnp.float32),
        "outer_momentum": normal_values(streams_of[6], (D, KV), 0.02, 0.3125, ((0, 16), (1, 32)), jnp.float32),
    }


beta_one = 0.9
beta_two = 0.95
adam_eps = 1e-08
learn_rate = 0.0003
decay_rate = 0.1
outer_rate = 0.7
outer_mu = 0.9
blend_keep = 0.5

def group_pass(operands):
    inputs, cotangents, weights = operands
    partials = jnp.einsum('ftd,ftk->fdk', inputs.astype(jnp.float32), cotangents.astype(jnp.float32))
    rounded = lax.optimization_barrier(partials.astype(jnp.bfloat16))
    gradient = lax.optimization_barrier(jnp.sum(rounded.astype(jnp.float32), axis=0))
    flat_cot = cotangents.reshape(-1, weights.shape[1])
    grad_in = jnp.dot(flat_cot, weights.T, preferred_element_type=jnp.float32).astype(jnp.bfloat16)
    return (gradient, grad_in)

def reference(layer_input, cotangent, local_weight, first_moment, second_moment, anchor, outer_momentum):
    inputs = layer_input.reshape(N_REPLICA, N_FSDP, TOK_DEV, D)
    cotangents = cotangent.reshape(N_REPLICA, N_FSDP, TOK_DEV, KV)
    gradient, grad_in = lax.map(group_pass, (inputs, cotangents, local_weight))
    input_grad = grad_in.reshape(N_REPLICA * N_FSDP * TOK_DEV, D)
    new_first = beta_one * first_moment + (1.0 - beta_one) * gradient
    new_second = beta_two * second_moment + (1.0 - beta_two) * gradient * gradient
    weights = local_weight.astype(jnp.float32)
    update = new_first / (jnp.sqrt(new_second) + adam_eps)
    inner = weights - learn_rate * (update + decay_rate * weights)
    weight_sum = lax.optimization_barrier(jnp.sum(weights, axis=0))
    delta = anchor - weight_sum / N_REPLICA
    new_momentum = outer_mu * outer_momentum + delta
    new_anchor = anchor - outer_rate * (delta + outer_mu * new_momentum)
    new_weight = (blend_keep * inner + (1.0 - blend_keep) * new_anchor[None]).astype(jnp.bfloat16)
    return (input_grad, new_weight, new_first, new_second, new_anchor, new_momentum)
```

```python
import jax
import jax.numpy as jnp
from jax import lax
from jax.experimental import pallas as pl
from jax.experimental.pallas import tpu as pltpu
from jax.sharding import PartitionSpec as P

beta_one = 0.9
beta_two = 0.95
adam_eps = 1e-08
learn_rate = 0.0003
decay_rate = 0.1
outer_rate = 0.7
outer_mu = 0.9
blend_keep = 0.5

MESH = pl.DeviceIdType.MESH
NY = 8
NZ = 8
TOK = 240
D = 3072
KV = 512
ROWS = 192
PAIR = 2 * ROWS
NPAIR = NY // 2
AG_SUBS = 2
RS_SUBS = 2
SHARE = 16
F32 = jnp.float32
BF16 = jnp.bfloat16


def mod(value, size):
    return lax.rem(value + size, size)


def dot(a, b, dims):
    return lax.dot_general(a, b, (dims, ((), ())), preferred_element_type=F32)


def step_kernel(
    x_ref, c_ref, w_ref, m1_ref, m2_ref, a_ref, om_ref,
    ig_own, ig_recv, nw_ref, nf_ref, ns_ref, na_ref, nm_ref,
    xo, xp, cm, cp, wf, part, sb0, sb, rb0, rb, igs, wt, r1, s1, r2, fa, an, om, m1, m2,
    local_sem, xs, xr, ag_s, ag_r, rs_s, rs_r, z1_s, z1_r, g2_s, g2_r, g3_s, g3_r, z4_s, z4_r,
):
    rep = lax.axis_index("replica")
    fs = lax.axis_index("fsdp")
    half, y = fs // NY, lax.rem(fs, NY)
    xh, z, core = rep // (NZ * 2), lax.rem(rep // 2, NZ), lax.rem(rep, 2)

    def rep_of(xh_, z_, core_):
        return (xh_ * NZ + z_) * 2 + core_

    partner = (rep, (1 - half) * NY + y)
    ring = ((rep, half * NY + mod(y + 1, NY)), (rep, half * NY + mod(y - 1, NY)))
    zs = [(rep_of(xh, mod(z + d, NZ), core), fs) for d in range(1, NZ)]
    group = [(rep_of(lax.rem(xh + j // 2, 2), z, lax.rem(core + j % 2, 2)), fs) for j in range(1, 4)]

    barrier = pltpu.get_barrier_semaphore()
    for peer in (partner, *ring, *zs, *group):
        pl.semaphore_signal(barrier, inc=1, device_id=peer, device_id_type=MESH)

    def remote(src, dst, send, recv, peer):
        return pltpu.make_async_remote_copy(src, dst, send, recv, device_id=peer, device_id_type=MESH)

    quad = y // 2
    odd = lax.rem(y, 2)
    order = [mod(quad + 2, NPAIR), mod(quad + 1 + 2 * odd, NPAIR), mod(quad + 3 + 2 * odd, NPAIR), quad]

    def pair_columns(which, pair):
        return pl.ds(pl.multiple_of(which * (D // 2) + pair * PAIR, 128), PAIR)

    def block(ref, b, rows):
        start = pl.multiple_of(lax.rem(b, 2) * ROWS + rows[0], 16)
        return ref.at[b // 2, pl.ds(start, rows[1])]

    load_w = pltpu.make_async_copy(w_ref, block(wf, y, (0, ROWS)), local_sem.at[0])
    load_c = pltpu.make_async_copy(c_ref, cm, local_sem.at[1])
    load_w.start()
    load_c.start()
    load_x = [
        pltpu.make_async_copy(x_ref.at[:, pair_columns(half, order[i])], xo.at[order[i]], local_sem.at[2 + i])
        for i in range(NPAIR)
    ]
    loads = [
        pltpu.make_async_copy(src, dst, local_sem.at[2 + NPAIR + i])
        for i, (src, dst) in enumerate(((a_ref, an), (om_ref, om), (m1_ref, m1), (m2_ref, m2)))
    ]
    for load in (*load_x, *loads):
        load.start()
    load_w.wait()
    eye = (
        lax.broadcasted_iota(jnp.int32, (KV, KV), 0) == lax.broadcasted_iota(jnp.int32, (KV, KV), 1)
    ).astype(BF16)
    own_w = block(wf, y, (0, ROWS))[...]
    wt[...] = dot(eye, own_w, ((1,), (1,))).astype(BF16).reshape(2, NZ, 2 * SHARE, ROWS)
    load_c.wait()
    pl.semaphore_wait(barrier, 3 + len(zs) + len(group))

    send_c = remote(cm, cp, xs.at[0], xr.at[0], partner)
    send_x = [
        remote(x_ref.at[:, pair_columns(1 - half, order[i])], xp.at[order[i]], xs.at[1 + i], xr.at[1 + i], partner)
        for i in range(NPAIR)
    ]
    send_ig = [
        remote(igs.at[i], ig_recv.at[i], xs.at[1 + NPAIR + i], xr.at[1 + NPAIR + i], partner) for i in range(NPAIR)
    ]

    sub = ROWS // AG_SUBS

    def ag(d, s, j):
        place = block(wf, mod(y - s, NY) if d == 0 else mod(y + s, NY), (j * sub, sub))
        return remote(place, place, ag_s.at[d, s, j], ag_r.at[d, s, j], ring[d])

    def ag_subs(d, s):
        if s < NY // 2 - 1:
            return range(AG_SUBS)
        return range(AG_SUBS // 2) if d == 0 else range(AG_SUBS // 2, AG_SUBS)

    send_c.start()
    for j in range(AG_SUBS):
        for d in range(2):
            ag(d, 0, j).start()
    for copy in send_x:
        copy.start()
    z1 = [
        remote(wt.at[:, mod(z + d, NZ)], r1.at[d - 1], z1_s.at[d - 1], z1_r.at[d - 1], zs[d - 1]) for d in range(1, NZ)
    ]
    for copy in z1:
        copy.start()

    def ag_forward(s):
        for j in range(AG_SUBS):
            for d in range(2):
                if j in ag_subs(d, s - 1):
                    ag(d, s - 1, j).wait_recv()
                if s < NY // 2 and j in ag_subs(d, s):
                    ag(d, s, j).start()

    rsub = ROWS // RS_SUBS

    def rs(d, s, j):
        rows = pl.ds(j * rsub, rsub)
        if s == 0:
            return remote(sb0.at[d, rows], rb0.at[d, rows], rs_s.at[d, s, j], rs_r.at[d, s, j], ring[d])
        return remote(sb.at[d, s - 1, rows], rb.at[d, s - 1, rows], rs_s.at[d, s, j], rs_r.at[d, s, j], ring[d])

    def rs_step(s):
        for j in range(RS_SUBS):
            rows = pl.ds(j * rsub, rsub)
            for d in range(2):
                dest = mod(y + 4 - s, NY) if d == 0 else mod(y - 4 + s, NY)
                own = block(part, dest, (j * rsub, rsub))
                near = pl.ds(d * (KV // 2), KV // 2)
                far = pl.ds((1 - d) * (KV // 2), KV // 2)
                if s == 0:
                    sb0[d, rows] = own[:, near].astype(BF16)
                elif s == 1:
                    rs(d, 0, j).wait_recv()
                    sb[d, 0, rows, near] = (own[:, near] + rb0[d, rows].astype(F32)).astype(BF16)
                    sb[d, 0, rows, far] = own[:, far].astype(BF16)
                else:
                    rs(d, s - 1, j).wait_recv()
                    sb[d, s - 1, rows] = (own[...] + rb[d, s - 2, rows].astype(F32)).astype(BF16)
                rs(d, s, j).start()

    def make_part(i):
        load_x[i].wait()
        send_x[i].wait_recv()
        part[order[i]] = dot(xo[order[i]], cm[...], ((0,), (0,))) + dot(xp[order[i]], cp[...], ((0,), (0,)))

    ag_forward(1)

    for copy in z1:
        copy.wait_recv()
    total = wt[:, pl.ds(z, 1)].astype(F32).reshape(2, 2 * SHARE, ROWS)
    for d in range(NZ - 1):
        total = total + r1[d].astype(F32)
    s1[...] = total.reshape(2, 2, SHARE, ROWS)
    g2 = [
        remote(
            s1.at[lax.rem(xh + j // 2, 2), lax.rem(core + j % 2, 2)], r2.at[j - 1],
            g2_s.at[j - 1], g2_r.at[j - 1], group[j - 1],
        )
        for j in range(1, 4)
    ]
    for copy in g2:
        copy.start()

    ag_forward(2)
    send_c.wait_recv()
    make_part(0)
    rs_step(0)

    for copy in g2:
        copy.wait_recv()
    for load in loads[:2]:
        load.wait()
    share = s1[pl.ds(xh, 1), pl.ds(core, 1)].reshape(SHARE, ROWS)
    share = share + r2[0] + r2[1] + r2[2]
    anchor = an[...]
    delta = anchor - share / (2 * NZ * 2)
    new_momentum = outer_mu * om[...] + delta
    new_anchor = anchor - outer_rate * (delta + outer_mu * new_momentum)
    nm_ref[...] = new_momentum
    na_ref[...] = new_anchor
    fa[pl.ds(xh, 1), pl.ds(z, 1), pl.ds(core, 1)] = new_anchor[None, None, None]
    mine = fa.at[xh, z, core]
    g3 = [remote(mine, mine, g3_s.at[j], g3_r.at[j], group[j]) for j in range(3)]
    for copy in g3:
        copy.start()

    ag_forward(3)
    make_part(1)
    rs_step(1)
    for copy in g3:
        copy.wait_recv()
    layer = fa.at[:, z]
    z4 = [remote(layer, layer, z4_s.at[d], z4_r.at[d], zs[d]) for d in range(NZ - 1)]
    for copy in z4:
        copy.start()

    ag_forward(4)
    for i in range(NPAIR):
        igs[i] = dot(cp[...], wf[i], ((1,), (1,))).astype(BF16)
        send_ig[i].start()

    make_part(2)
    rs_step(2)
    make_part(3)
    rs_step(3)
    for i in range(NPAIR):
        ig_own[i] = dot(cm[...], wf[i], ((1,), (1,))).astype(BF16)

    for load in loads[2:]:
        load.wait()
    for copy in z4:
        copy.wait_recv()
    full_anchor = fa[...].reshape(KV, ROWS).T
    for j in range(RS_SUBS):
        rows = pl.ds(j * rsub, rsub)
        for d in range(2):
            rs(d, 3, j).wait_recv()
        gradient = block(part, y, (j * rsub, rsub))[...] + rb[0, 2, rows].astype(F32) + rb[1, 2, rows].astype(F32)
        new_first = beta_one * m1[rows] + (1.0 - beta_one) * gradient
        new_second = beta_two * m2[rows] + (1.0 - beta_two) * gradient * gradient
        nf_ref[rows] = new_first
        ns_ref[rows] = new_second
        weights = block(wf, y, (j * rsub, rsub))[...].astype(F32)
        update = new_first / (jnp.sqrt(new_second) + adam_eps)
        inner = weights - learn_rate * (update + decay_rate * weights)
        blend = blend_keep * inner + (1.0 - blend_keep) * full_anchor[j * rsub : (j + 1) * rsub]
        nw_ref[rows] = blend.astype(BF16)

    for copy in send_ig:
        copy.wait_recv()
    for copy in (send_c, *send_x, *send_ig, *z1, *g2, *g3, *z4):
        copy.wait_send()
    for s in range(NY // 2):
        for d in range(2):
            for j in ag_subs(d, s):
                ag(d, s, j).wait_send()
            for j in range(RS_SUBS):
                rs(d, s, j).wait_send()


def write_kernel(half_ref, ig_own, ig_recv, nw, nf, ns, na, nm, o_ig, o_nw, o_nf, o_ns, o_na, o_nm, sem):
    half = half_ref[0]
    copies = []
    for i in range(NPAIR):
        for which, source in ((half, ig_own), (1 - half, ig_recv)):
            columns = pl.ds(pl.multiple_of(which * (D // 2) + i * PAIR, 128), PAIR)
            copies.append((source.at[i], o_ig.at[:, columns]))
    copies += [(nw, o_nw), (nf, o_nf), (ns, o_ns), (na, o_na), (nm, o_nm)]
    copies = [pltpu.make_async_copy(src, dst, sem.at[k]) for k, (src, dst) in enumerate(copies)]
    for copy in copies:
        copy.start()
    for copy in copies:
        copy.wait()


def body(layer_input, cotangent, local_weight, first_moment, second_moment, anchor, outer_momentum):
    vmem = pl.BlockSpec(memory_space=pltpu.VMEM)
    hbm = pl.BlockSpec(memory_space=pl.ANY)
    shape = jax.ShapeDtypeStruct
    dma = pltpu.SemaphoreType.DMA
    small = shape((SHARE, ROWS), F32)
    wide = shape((ROWS, KV), F32)
    results = pl.pallas_call(
        step_kernel,
        out_shape=(
            shape((NPAIR, TOK, PAIR), BF16), shape((NPAIR, TOK, PAIR), BF16),
            shape((ROWS, KV), BF16), wide, wide, small, small,
        ),
        in_specs=[hbm] * 7,
        out_specs=[vmem] * 7,
        scratch_shapes=[
            pltpu.VMEM((NPAIR, TOK, PAIR), BF16),
            pltpu.VMEM((NPAIR, TOK, PAIR), BF16),
            pltpu.VMEM((TOK, KV), BF16),
            pltpu.VMEM((TOK, KV), BF16),
            pltpu.VMEM((NPAIR, PAIR, KV), BF16),
            pltpu.VMEM((NPAIR, PAIR, KV), F32),
            pltpu.VMEM((2, ROWS, KV // 2), BF16),
            pltpu.VMEM((2, 3, ROWS, KV), BF16),
            pltpu.VMEM((2, ROWS, KV // 2), BF16),
            pltpu.VMEM((2, 3, ROWS, KV), BF16),
            pltpu.VMEM((NPAIR, TOK, PAIR), BF16),
            pltpu.VMEM((2, NZ, 2 * SHARE, ROWS), BF16),
            pltpu.VMEM((NZ - 1, 2, 2 * SHARE, ROWS), BF16),
            pltpu.VMEM((2, 2, SHARE, ROWS), F32),
            pltpu.VMEM((3, SHARE, ROWS), F32),
            pltpu.VMEM((2, NZ, 2, SHARE, ROWS), F32),
            pltpu.VMEM((SHARE, ROWS), F32),
            pltpu.VMEM((SHARE, ROWS), F32),
            pltpu.VMEM((ROWS, KV), F32),
            pltpu.VMEM((ROWS, KV), F32),
            dma((2 + NPAIR + 4,)),
            dma((1 + 2 * NPAIR,)), dma((1 + 2 * NPAIR,)),
            dma((2, NY // 2, AG_SUBS)), dma((2, NY // 2, AG_SUBS)),
            dma((2, NY // 2, RS_SUBS)), dma((2, NY // 2, RS_SUBS)),
            dma((NZ - 1,)), dma((NZ - 1,)),
            dma((3,)), dma((3,)),
            dma((3,)), dma((3,)),
            dma((NZ - 1,)), dma((NZ - 1,)),
        ],
        compiler_params=pltpu.CompilerParams(
            collective_id=0, has_side_effects=True, vmem_limit_bytes=40 << 20
        ),
        cost_estimate=pl.CostEstimate(flops=1_600_000_000, bytes_accessed=5_000_000, transcendentals=200_000),
        name="step",
    )(
        layer_input, cotangent, local_weight[0], first_moment[0], second_moment[0], anchor.T, outer_momentum.T
    )
    half = (lax.axis_index("fsdp") // NY).astype(jnp.int32).reshape(1)
    outs = pl.pallas_call(
        write_kernel,
        out_shape=(shape((TOK, D), BF16), shape((ROWS, KV), BF16), wide, wide, small, small),
        in_specs=[pl.BlockSpec(memory_space=pltpu.SMEM)] + [vmem] * 7,
        out_specs=[hbm] * 6,
        scratch_shapes=[dma((2 * NPAIR + 5,))],
        name="write",
    )(half, *results)
    input_grad, new_weight, new_first, new_second, new_anchor, new_momentum = outs
    return input_grad, new_weight[None], new_first[None], new_second[None], new_anchor.T, new_momentum.T


def solution(mesh):
    in_specs = (
        P(("replica", "fsdp"), None),
        P(("replica", "fsdp"), None),
        P("replica", "fsdp", None),
        P("replica", "fsdp", None),
        P("replica", "fsdp", None),
        P("fsdp", "replica"),
        P("fsdp", "replica"),
    )
    out_specs = (
        P(("replica", "fsdp"), None),
        P("replica", "fsdp", None),
        P("replica", "fsdp", None),
        P("replica", "fsdp", None),
        P("fsdp", "replica"),
        P("fsdp", "replica"),
    )
    return jax.shard_map(body, mesh=mesh, in_specs=in_specs, out_specs=out_specs, check_vma=False)
```

```python
import jax
import jax.numpy as jnp
from jax import lax
from jax.experimental import pallas as pl
from jax.experimental.pallas import tpu as pltpu
from jax.sharding import PartitionSpec as P

beta_one = 0.9
beta_two = 0.95
adam_eps = 1e-08
learn_rate = 0.0003
decay_rate = 0.1
outer_rate = 0.7
outer_mu = 0.9
blend_keep = 0.5

MESH = pl.DeviceIdType.MESH
NY = 8
NZ = 8
TOK = 240
D = 3072
KV = 512
ROWS = 192
PAIR = 2 * ROWS
NPAIR = NY // 2
AG_SUBS = 2
RS_SUBS = 2
MID = 128
SIDE = PAIR - MID
SHARE = 16
F32 = jnp.float32
BF16 = jnp.bfloat16


def mod(value, size):
    return lax.rem(value + size, size)


def dot(a, b, dims):
    return lax.dot_general(a, b, (dims, ((), ())), preferred_element_type=F32)


def step_kernel(
    x_ref, c_ref, w_ref, m1_ref, m2_ref, a_ref, om_ref,
    ig_own, ig_recv, ig_mid, nw_ref, nf_ref, ns_ref, na_ref, nm_ref,
    xo, xp, cm, cp, wf, wo, part, sb0, sb, rb0, rb, igs, wt, r1, s1, r2, fa, an, om, m1, m2,
    local_sem, xs, xr, ag_s, ag_r, mid_s, mid_r, rs_s, rs_r, z1_s, z1_r, g2_s, g2_r, g3_s, g3_r, z4_s, z4_r,
):
    rep = lax.axis_index("replica")
    fs = lax.axis_index("fsdp")
    half, y = fs // NY, lax.rem(fs, NY)
    xh, z, core = rep // (NZ * 2), lax.rem(rep // 2, NZ), lax.rem(rep, 2)

    def rep_of(xh_, z_, core_):
        return (xh_ * NZ + z_) * 2 + core_

    partner = (rep, (1 - half) * NY + y)
    ring = ((rep, half * NY + mod(y + 1, NY)), (rep, half * NY + mod(y - 1, NY)))
    zs = [(rep_of(xh, mod(z + d, NZ), core), fs) for d in range(1, NZ)]
    group = [(rep_of(lax.rem(xh + j // 2, 2), z, lax.rem(core + j % 2, 2)), fs) for j in range(1, 4)]

    barrier = pltpu.get_barrier_semaphore()
    for peer in (partner, *ring, *zs, *group):
        pl.semaphore_signal(barrier, inc=1, device_id=peer, device_id_type=MESH)

    def remote(src, dst, send, recv, peer):
        return pltpu.make_async_remote_copy(src, dst, send, recv, device_id=peer, device_id_type=MESH)

    quad = y // 2
    odd = lax.rem(y, 2)
    order = [mod(quad + 2, NPAIR), mod(quad + 1 + 2 * odd, NPAIR), mod(quad + 3 + 2 * odd, NPAIR), quad]

    def pair_columns(which, pair):
        return pl.ds(pl.multiple_of(which * (D // 2) + pair * PAIR, 128), PAIR)

    def block(ref, b, rows):
        start = pl.multiple_of(lax.rem(b, 2) * ROWS + rows[0], 16)
        return ref.at[b // 2, pl.ds(start, rows[1])]

    load_w = pltpu.make_async_copy(w_ref, block(wf, y, (0, ROWS)), local_sem.at[0])
    load_c = pltpu.make_async_copy(c_ref, cm, local_sem.at[1])
    load_w.start()
    load_c.start()
    load_x = [
        pltpu.make_async_copy(x_ref.at[:, pair_columns(half, order[i])], xo.at[order[i]], local_sem.at[2 + i])
        for i in range(NPAIR)
    ]
    loads = [
        pltpu.make_async_copy(src, dst, local_sem.at[2 + NPAIR + i])
        for i, (src, dst) in enumerate(((a_ref, an), (om_ref, om), (m1_ref, m1), (m2_ref, m2)))
    ]
    for load in (*load_x, *loads):
        load.start()
    load_w.wait()
    eye = (
        lax.broadcasted_iota(jnp.int32, (KV, KV), 0) == lax.broadcasted_iota(jnp.int32, (KV, KV), 1)
    ).astype(BF16)
    own_w = block(wf, y, (0, ROWS))[...]
    wt[...] = dot(eye, own_w, ((1,), (1,))).astype(BF16).reshape(2, NZ, 2 * SHARE, ROWS)
    load_c.wait()
    pl.semaphore_wait(barrier, 3 + len(zs) + len(group))

    send_c = remote(cm, cp, xs.at[0], xr.at[0], partner)
    send_x = [
        remote(x_ref.at[:, pair_columns(1 - half, order[i])], xp.at[order[i]], xs.at[1 + i], xr.at[1 + i], partner)
        for i in range(NPAIR)
    ]
    send_ig = [
        remote(igs.at[i], ig_recv.at[i], xs.at[1 + NPAIR + i], xr.at[1 + NPAIR + i], partner) for i in range(NPAIR)
    ]

    sub = ROWS // AG_SUBS

    def ag(d, s, j):
        place = block(wf, mod(y - s, NY) if d == 0 else mod(y + s, NY), (j * sub, sub))
        return remote(place, place, ag_s.at[d, s, j], ag_r.at[d, s, j], ring[d])

    def ag_subs(d, s):
        if s < NY // 2 - 1:
            return range(AG_SUBS)
        return range(AG_SUBS // 2) if d == 0 else range(AG_SUBS // 2, AG_SUBS)

    middle = pl.ds(pl.multiple_of(MID // 2 * odd, 16), MID // 2)
    send_mid = remote(
        wf.at[quad, pl.ds(pl.multiple_of(MID + MID // 2 * odd, 16), MID // 2)], wo.at[quad, middle],
        xs.at[1 + 2 * NPAIR], xr.at[1 + 2 * NPAIR], partner,
    )

    def mid(d, s):
        b = mod(y - s, NY) if d == 0 else mod(y + s, NY)
        start, size = (0, MID // 2) if s < NY // 2 - 1 else (d * (MID // 4), MID // 4)
        place = wo.at[b // 2, pl.ds(pl.multiple_of(lax.rem(b, 2) * (MID // 2) + start, 16), size)]
        return remote(place, place, mid_s.at[d, s], mid_r.at[d, s], ring[d])

    def mid_forward(s):
        for d in range(2):
            if s > 0:
                mid(d, s - 1).wait_recv()
            if s < NY // 2:
                mid(d, s).start()

    send_mid.start()
    send_c.start()
    for j in range(AG_SUBS):
        for d in range(2):
            ag(d, 0, j).start()
    send_x[0].start()
    z1 = [
        remote(wt.at[:, mod(z + d, NZ)], r1.at[d - 1], z1_s.at[d - 1], z1_r.at[d - 1], zs[d - 1]) for d in range(1, NZ)
    ]
    for copy in z1:
        copy.start()

    def ag_forward(s):
        for j in range(AG_SUBS):
            for d in range(2):
                if j in ag_subs(d, s - 1):
                    ag(d, s - 1, j).wait_recv()
                if s < NY // 2 and j in ag_subs(d, s):
                    ag(d, s, j).start()

    rsub = ROWS // RS_SUBS

    def rs(d, s, j):
        rows = pl.ds(j * rsub, rsub)
        if s == 0:
            return remote(sb0.at[d, rows], rb0.at[d, rows], rs_s.at[d, s, j], rs_r.at[d, s, j], ring[d])
        return remote(sb.at[d, s - 1, rows], rb.at[d, s - 1, rows], rs_s.at[d, s, j], rs_r.at[d, s, j], ring[d])

    def rs_step(s):
        for j in range(RS_SUBS):
            rows = pl.ds(j * rsub, rsub)
            for d in range(2):
                dest = mod(y + 4 - s, NY) if d == 0 else mod(y - 4 + s, NY)
                own = block(part, dest, (j * rsub, rsub))
                near = pl.ds(d * (KV // 2), KV // 2)
                far = pl.ds((1 - d) * (KV // 2), KV // 2)
                if s == 0:
                    sb0[d, rows] = own[:, near].astype(BF16)
                elif s == 1:
                    rs(d, 0, j).wait_recv()
                    sb[d, 0, rows, near] = (own[:, near] + rb0[d, rows].astype(F32)).astype(BF16)
                    sb[d, 0, rows, far] = own[:, far].astype(BF16)
                else:
                    rs(d, s - 1, j).wait_recv()
                    sb[d, s - 1, rows] = (own[...] + rb[d, s - 2, rows].astype(F32)).astype(BF16)
                rs(d, s, j).start()

    def make_part(i):
        load_x[i].wait()
        send_x[i].wait_recv()
        part[order[i]] = dot(xo[order[i]], cm[...], ((0,), (0,))) + dot(xp[order[i]], cp[...], ((0,), (0,)))

    ag_forward(1)
    send_mid.wait_recv()
    mid_forward(0)

    for copy in z1:
        copy.wait_recv()
    total = wt[:, pl.ds(z, 1)].astype(F32).reshape(2, 2 * SHARE, ROWS)
    for d in range(NZ - 1):
        total = total + r1[d].astype(F32)
    s1[...] = total.reshape(2, 2, SHARE, ROWS)
    g2 = [
        remote(
            s1.at[lax.rem(xh + j // 2, 2), lax.rem(core + j % 2, 2)], r2.at[j - 1],
            g2_s.at[j - 1], g2_r.at[j - 1], group[j - 1],
        )
        for j in range(1, 4)
    ]
    for copy in g2:
        copy.start()
    send_x[1].start()

    ag_forward(2)
    mid_forward(1)
    send_c.wait_recv()
    make_part(0)
    rs_step(0)
    send_x[2].start()

    for copy in g2:
        copy.wait_recv()
    for load in loads[:2]:
        load.wait()
    share = s1[pl.ds(xh, 1), pl.ds(core, 1)].reshape(SHARE, ROWS)
    share = share + r2[0] + r2[1] + r2[2]
    anchor = an[...]
    delta = anchor - share / (2 * NZ * 2)
    new_momentum = outer_mu * om[...] + delta
    new_anchor = anchor - outer_rate * (delta + outer_mu * new_momentum)
    nm_ref[...] = new_momentum
    na_ref[...] = new_anchor
    fa[pl.ds(xh, 1), pl.ds(z, 1), pl.ds(core, 1)] = new_anchor[None, None, None]
    mine = fa.at[xh, z, core]
    g3 = [remote(mine, mine, g3_s.at[j], g3_r.at[j], group[j]) for j in range(3)]
    for copy in g3:
        copy.start()
    send_x[3].start()

    ag_forward(3)
    mid_forward(2)
    make_part(1)
    rs_step(1)
    for copy in g3:
        copy.wait_recv()
    layer = fa.at[:, z]
    z4 = [remote(layer, layer, z4_s.at[d], z4_r.at[d], zs[d]) for d in range(NZ - 1)]
    for copy in z4:
        copy.start()

    ag_forward(4)
    mid_forward(3)
    for i in range(NPAIR):
        for k, rows in enumerate((pl.ds(0, SIDE // 2), pl.ds(PAIR - SIDE // 2, SIDE // 2))):
            igs[i, :, k * (SIDE // 2) : (k + 1) * (SIDE // 2)] = dot(cp[...], wf[i, rows], ((1,), (1,))).astype(BF16)
        send_ig[i].start()

    make_part(2)
    rs_step(2)
    make_part(3)
    rs_step(3)
    for i in range(NPAIR):
        ig_own[i] = dot(cm[...], wf[i], ((1,), (1,))).astype(BF16)
    mid_forward(4)
    for i in range(NPAIR):
        ig_mid[i] = dot(cm[...], wo[i], ((1,), (1,))).astype(BF16)

    for load in loads[2:]:
        load.wait()
    for copy in z4:
        copy.wait_recv()
    full_anchor = fa[...].reshape(KV, ROWS).T
    for j in range(RS_SUBS):
        rows = pl.ds(j * rsub, rsub)
        for d in range(2):
            rs(d, 3, j).wait_recv()
        gradient = block(part, y, (j * rsub, rsub))[...] + rb[0, 2, rows].astype(F32) + rb[1, 2, rows].astype(F32)
        new_first = beta_one * m1[rows] + (1.0 - beta_one) * gradient
        new_second = beta_two * m2[rows] + (1.0 - beta_two) * gradient * gradient
        nf_ref[rows] = new_first
        ns_ref[rows] = new_second
        weights = block(wf, y, (j * rsub, rsub))[...].astype(F32)
        update = new_first / (jnp.sqrt(new_second) + adam_eps)
        inner = weights - learn_rate * (update + decay_rate * weights)
        blend = blend_keep * inner + (1.0 - blend_keep) * full_anchor[j * rsub : (j + 1) * rsub]
        nw_ref[rows] = blend.astype(BF16)

    for copy in send_ig:
        copy.wait_recv()
    for copy in (send_mid, send_c, *send_x, *send_ig, *z1, *g2, *g3, *z4):
        copy.wait_send()
    for s in range(NY // 2):
        for d in range(2):
            mid(d, s).wait_send()
            for j in ag_subs(d, s):
                ag(d, s, j).wait_send()
            for j in range(RS_SUBS):
                rs(d, s, j).wait_send()


def write_kernel(half_ref, ig_own, ig_recv, ig_mid, nw, nf, ns, na, nm, o_ig, o_nw, o_nf, o_ns, o_na, o_nm, sem):
    half = half_ref[0]
    copies = []
    for i in range(NPAIR):
        for which, source, start, size in (
            (half, ig_own.at[i], 0, PAIR),
            (1 - half, ig_recv.at[i, :, pl.ds(0, SIDE // 2)], 0, SIDE // 2),
            (1 - half, ig_mid.at[i], SIDE // 2, MID),
            (1 - half, ig_recv.at[i, :, pl.ds(SIDE // 2, SIDE // 2)], SIDE // 2 + MID, SIDE // 2),
        ):
            columns = pl.ds(pl.multiple_of(which * (D // 2) + i * PAIR + start, 128), size)
            copies.append((source, o_ig.at[:, columns]))
    copies += [(nw, o_nw), (nf, o_nf), (ns, o_ns), (na, o_na), (nm, o_nm)]
    copies = [pltpu.make_async_copy(src, dst, sem.at[k]) for k, (src, dst) in enumerate(copies)]
    for copy in copies:
        copy.start()
    for copy in copies:
        copy.wait()


def body(layer_input, cotangent, local_weight, first_moment, second_moment, anchor, outer_momentum):
    vmem = pl.BlockSpec(memory_space=pltpu.VMEM)
    hbm = pl.BlockSpec(memory_space=pl.ANY)
    shape = jax.ShapeDtypeStruct
    dma = pltpu.SemaphoreType.DMA
    small = shape((SHARE, ROWS), F32)
    wide = shape((ROWS, KV), F32)
    results = pl.pallas_call(
        step_kernel,
        out_shape=(
            shape((NPAIR, TOK, PAIR), BF16), shape((NPAIR, TOK, SIDE), BF16), shape((NPAIR, TOK, MID), BF16),
            shape((ROWS, KV), BF16), wide, wide, small, small,
        ),
        in_specs=[hbm] * 7,
        out_specs=[vmem] * 8,
        scratch_shapes=[
            pltpu.VMEM((NPAIR, TOK, PAIR), BF16),
            pltpu.VMEM((NPAIR, TOK, PAIR), BF16),
            pltpu.VMEM((TOK, KV), BF16),
            pltpu.VMEM((TOK, KV), BF16),
            pltpu.VMEM((NPAIR, PAIR, KV), BF16),
            pltpu.VMEM((NPAIR, MID, KV), BF16),
            pltpu.VMEM((NPAIR, PAIR, KV), F32),
            pltpu.VMEM((2, ROWS, KV // 2), BF16),
            pltpu.VMEM((2, 3, ROWS, KV), BF16),
            pltpu.VMEM((2, ROWS, KV // 2), BF16),
            pltpu.VMEM((2, 3, ROWS, KV), BF16),
            pltpu.VMEM((NPAIR, TOK, SIDE), BF16),
            pltpu.VMEM((2, NZ, 2 * SHARE, ROWS), BF16),
            pltpu.VMEM((NZ - 1, 2, 2 * SHARE, ROWS), BF16),
            pltpu.VMEM((2, 2, SHARE, ROWS), F32),
            pltpu.VMEM((3, SHARE, ROWS), F32),
            pltpu.VMEM((2, NZ, 2, SHARE, ROWS), F32),
            pltpu.VMEM((SHARE, ROWS), F32),
            pltpu.VMEM((SHARE, ROWS), F32),
            pltpu.VMEM((ROWS, KV), F32),
            pltpu.VMEM((ROWS, KV), F32),
            dma((2 + NPAIR + 4,)),
            dma((2 + 2 * NPAIR,)), dma((2 + 2 * NPAIR,)),
            dma((2, NY // 2, AG_SUBS)), dma((2, NY // 2, AG_SUBS)),
            dma((2, NY // 2)), dma((2, NY // 2)),
            dma((2, NY // 2, RS_SUBS)), dma((2, NY // 2, RS_SUBS)),
            dma((NZ - 1,)), dma((NZ - 1,)),
            dma((3,)), dma((3,)),
            dma((3,)), dma((3,)),
            dma((NZ - 1,)), dma((NZ - 1,)),
        ],
        compiler_params=pltpu.CompilerParams(
            collective_id=0, has_side_effects=True, vmem_limit_bytes=40 << 20
        ),
        cost_estimate=pl.CostEstimate(flops=1_600_000_000, bytes_accessed=5_000_000, transcendentals=200_000),
        name="step",
    )(
        *(
            pltpu.with_memory_space_constraint(array, pltpu.HBM)
            for array in (
                layer_input, cotangent, local_weight[0], first_moment[0], second_moment[0], anchor.T, outer_momentum.T
            )
        )
    )
    half = (lax.axis_index("fsdp") // NY).astype(jnp.int32).reshape(1)
    outs = pl.pallas_call(
        write_kernel,
        out_shape=(shape((TOK, D), BF16), shape((ROWS, KV), BF16), wide, wide, small, small),
        in_specs=[pl.BlockSpec(memory_space=pltpu.SMEM)] + [vmem] * 8,
        out_specs=[hbm] * 6,
        scratch_shapes=[dma((4 * NPAIR + 5,))],
        name="write",
    )(half, *(pltpu.with_memory_space_constraint(array, pltpu.VMEM) for array in results))
    input_grad, new_weight, new_first, new_second, new_anchor, new_momentum = outs
    return input_grad, new_weight[None], new_first[None], new_second[None], new_anchor.T, new_momentum.T


def solution(mesh):
    in_specs = (
        P(("replica", "fsdp"), None),
        P(("replica", "fsdp"), None),
        P("replica", "fsdp", None),
        P("replica", "fsdp", None),
        P("replica", "fsdp", None),
        P("fsdp", "replica"),
        P("fsdp", "replica"),
    )
    out_specs = (
        P(("replica", "fsdp"), None),
        P("replica", "fsdp", None),
        P("replica", "fsdp", None),
        P("replica", "fsdp", None),
        P("fsdp", "replica"),
        P("fsdp", "replica"),
    )
    return jax.shard_map(body, mesh=mesh, in_specs=in_specs, out_specs=out_specs, check_vma=False)
```

```python
import jax
import jax.numpy as jnp
from jax import lax
from jax.experimental import pallas as pl
from jax.experimental.pallas import tpu as pltpu
from jax.sharding import PartitionSpec as P

beta_one = 0.9
beta_two = 0.95
adam_eps = 1e-08
learn_rate = 0.0003
decay_rate = 0.1
outer_rate = 0.7
outer_mu = 0.9
blend_keep = 0.5

MESH = pl.DeviceIdType.MESH
NY = 8
NZ = 8
TOK = 240
D = 3072
KV = 512
ROWS = 192
PAIR = 2 * ROWS
NPAIR = NY // 2
AG_SUBS = 2
RS_SUBS = 2
MID = 128
SIDE = PAIR - MID
SHARE = 16
F32 = jnp.float32
BF16 = jnp.bfloat16


def mod(value, size):
    return lax.rem(value + size, size)


def dot(a, b, dims):
    return lax.dot_general(a, b, (dims, ((), ())), preferred_element_type=F32)


def step_kernel(
    x_ref, c_ref, w_ref, m1_ref, m2_ref, a_ref, om_ref,
    ig_own, ig_recv, ig_mid, nw_ref, nf_ref, ns_ref, na_ref, nm_ref,
    xo, xp, cm, cp, wf, wo, part, sb0, sb, rb0, rb, igs, wt, r1, s1, r2, s2, r3, ao, aop, fa, m1, m2,
    local_sem, xs, xr, ag_s, ag_r, mid_s, mid_r, rs_s, rs_r, z1_s, z1_r, z4_s, z4_r, g_s, g_r, hello, ready,
):
    rep = lax.axis_index("replica")
    fs = lax.axis_index("fsdp")
    half, y = fs // NY, lax.rem(fs, NY)
    xh, z, core = rep // (NZ * 2), lax.rem(rep // 2, NZ), lax.rem(rep, 2)

    def rep_of(xh_, z_, core_):
        return (xh_ * NZ + z_) * 2 + core_

    partner = (rep, (1 - half) * NY + y)
    ring = ((rep, half * NY + mod(y + 1, NY)), (rep, half * NY + mod(y - 1, NY)))
    zs = [(rep_of(xh, mod(z + d, NZ), core), fs) for d in range(1, NZ)]
    twin = (rep_of(xh, z, 1 - core), fs)
    other = (rep_of(1 - xh, z, core), fs)
    near = (partner, *ring, twin, other)
    white = lax.rem(half + y + core + xh, 2) == 0

    def signal(sem, peer):
        pl.semaphore_signal(sem, inc=1, device_id=peer, device_id_type=MESH)

    barrier = pltpu.get_barrier_semaphore()

    @pl.when(jnp.logical_not(white))
    def _():
        for peer in near:
            signal(barrier, peer)

    def remote(src, dst, send, recv, peer):
        return pltpu.make_async_remote_copy(src, dst, send, recv, device_id=peer, device_id_type=MESH)

    quad = y // 2
    odd = lax.rem(y, 2)
    order = [mod(quad + 2, NPAIR), mod(quad + 1 + 2 * odd, NPAIR), mod(quad + 3 + 2 * odd, NPAIR), quad]

    def pair_columns(which, pair):
        return pl.ds(pl.multiple_of(which * (D // 2) + pair * PAIR, 128), PAIR)

    def block(ref, b, rows):
        start = pl.multiple_of(lax.rem(b, 2) * ROWS + rows[0], 16)
        return ref.at[b // 2, pl.ds(start, rows[1])]

    load_w = pltpu.make_async_copy(w_ref, block(wf, y, (0, ROWS)), local_sem.at[0])
    load_c = pltpu.make_async_copy(c_ref, cm, local_sem.at[1])
    load_w.start()
    load_c.start()
    load_x = [
        pltpu.make_async_copy(x_ref.at[:, pair_columns(half, order[i])], xo.at[order[i]], local_sem.at[2 + i])
        for i in range(NPAIR)
    ]
    loads = [
        pltpu.make_async_copy(src, dst, local_sem.at[2 + NPAIR + i])
        for i, (src, dst) in enumerate(((a_ref, ao.at[0]), (om_ref, ao.at[1]), (m1_ref, m1), (m2_ref, m2)))
    ]
    for load in (*loads[:2], *load_x, *loads[2:]):
        load.start()
    load_w.wait()
    load_c.wait()
    for load in loads[:2]:
        load.wait()

    @pl.when(white)
    def _():
        pl.semaphore_wait(barrier, len(near))
        for peer in near:
            signal(hello, peer)

    @pl.when(jnp.logical_not(white))
    def _():
        pl.semaphore_wait(hello, len(near))
        for peer in zs:
            signal(barrier, peer)

    send_c = remote(cm, cp, xs.at[0], xr.at[0], partner)
    send_x = [
        remote(x_ref.at[:, pair_columns(1 - half, order[i])], xp.at[order[i]], xs.at[1 + i], xr.at[1 + i], partner)
        for i in range(NPAIR)
    ]
    send_ig = [
        remote(igs.at[i], ig_recv.at[i], xs.at[1 + NPAIR + i], xr.at[1 + NPAIR + i], partner) for i in range(NPAIR)
    ]

    sub = ROWS // AG_SUBS

    def ag(d, s, j):
        place = block(wf, mod(y - s, NY) if d == 0 else mod(y + s, NY), (j * sub, sub))
        return remote(place, place, ag_s.at[d, s, j], ag_r.at[d, s, j], ring[d])

    def ag_subs(d, s):
        if s < NY // 2 - 1:
            return range(AG_SUBS)
        return range(AG_SUBS // 2) if d == 0 else range(AG_SUBS // 2, AG_SUBS)

    def ag_forward(s, js=range(AG_SUBS)):
        for j in js:
            for d in range(2):
                if s > 0 and j in ag_subs(d, s - 1):
                    ag(d, s - 1, j).wait_recv()
                if s < NY // 2 and j in ag_subs(d, s):
                    ag(d, s, j).start()

    middle = pl.ds(pl.multiple_of(MID // 2 * odd, 16), MID // 2)
    send_mid = remote(
        wf.at[quad, pl.ds(pl.multiple_of(MID + MID // 2 * odd, 16), MID // 2)], wo.at[quad, middle],
        xs.at[1 + 2 * NPAIR], xr.at[1 + 2 * NPAIR], partner,
    )

    def mid(d, s):
        b = mod(y - s, NY) if d == 0 else mod(y + s, NY)
        start, size = (0, MID // 2) if s < NY // 2 - 1 else (d * (MID // 4), MID // 4)
        place = wo.at[b // 2, pl.ds(pl.multiple_of(lax.rem(b, 2) * (MID // 2) + start, 16), size)]
        return remote(place, place, mid_s.at[d, s], mid_r.at[d, s], ring[d])

    def mid_forward(s):
        if s == 0:
            send_mid.wait_recv()
        for d in range(2):
            if s > 0:
                mid(d, s - 1).wait_recv()
            if s < NY // 2:
                mid(d, s).start()

    rsub = ROWS // RS_SUBS

    def rs(d, s, j):
        rows = pl.ds(j * rsub, rsub)
        if s == 0:
            return remote(sb0.at[d, rows], rb0.at[d, rows], rs_s.at[d, s, j], rs_r.at[d, s, j], ring[d])
        return remote(sb.at[d, s - 1, rows], rb.at[d, s - 1, rows], rs_s.at[d, s, j], rs_r.at[d, s, j], ring[d])

    def rs_step(s, js=range(RS_SUBS)):
        for j in js:
            rows = pl.ds(j * rsub, rsub)
            for d in range(2):
                dest = mod(y + 4 - s, NY) if d == 0 else mod(y - 4 + s, NY)
                own = block(part, dest, (j * rsub, rsub))
                here = pl.ds(d * (KV // 2), KV // 2)
                there = pl.ds((1 - d) * (KV // 2), KV // 2)
                if s == 0:
                    sb0[d, rows] = own[:, here].astype(BF16)
                elif s == 1:
                    rs(d, 0, j).wait_recv()
                    sb[d, 0, rows, here] = (own[:, here] + rb0[d, rows].astype(F32)).astype(BF16)
                    sb[d, 0, rows, there] = own[:, there].astype(BF16)
                else:
                    rs(d, s - 1, j).wait_recv()
                    sb[d, s - 1, rows] = (own[...] + rb[d, s - 2, rows].astype(F32)).astype(BF16)
                rs(d, s, j).start()

    def make_part(i):
        if i == 0:
            send_c.wait_recv()
        load_x[i].wait()
        send_x[i].wait_recv()
        part[order[i]] = dot(xo[order[i]], cm[...], ((0,), (0,))) + dot(xp[order[i]], cp[...], ((0,), (0,)))

    z1 = [remote(wt.at[mod(z + d, NZ)], r1.at[d - 1], z1_s.at[d - 1], z1_r.at[d - 1], zs[d - 1]) for d in range(1, NZ)]
    g2 = remote(s1.at[1 - core], r2, g_s.at[0], g_r.at[0], twin)
    g3 = remote(s2, r3, g_s.at[1], g_r.at[1], other)
    mine = fa.at[z, core]
    z4 = [remote(mine, mine, z4_s.at[d], z4_r.at[d], zs[d]) for d in range(NZ - 1)]
    g5 = remote(fa.at[:, core], fa.at[:, core], g_s.at[2], g_r.at[2], twin)
    swap = remote(ao, aop, g_s.at[3], g_r.at[3], other)

    def transpose_weight():
        size = KV // 2
        eye = (
            lax.broadcasted_iota(jnp.int32, (size, size), 0) == lax.broadcasted_iota(jnp.int32, (size, size), 1)
        ).astype(BF16)
        own_w = block(wf, y, (0, ROWS))[...]
        stacked = jnp.concatenate([own_w[:, :size], own_w[:, size:]], axis=0)
        wt[...] = dot(eye, stacked, ((1,), (1,))).astype(BF16).reshape(NZ, 2 * SHARE, 2 * ROWS)

    def z_ready():
        @pl.when(jnp.logical_not(white))
        def _():
            pl.semaphore_wait(barrier, len(zs))
            signal(ready, partner)

        @pl.when(white)
        def _():
            pl.semaphore_wait(ready, 1)

        for copy in z1:
            copy.start()

    def sum_z():
        for copy in z1:
            copy.wait_recv()
        total = wt[z].astype(F32)
        for d in range(NZ - 1):
            total = total + r1[d].astype(F32)
        s1[...] = total.reshape(2, SHARE, 2 * ROWS)
        g2.start()

    def sum_core():
        g2.wait_recv()
        s2[...] = s1[core] + r2[...]
        g3.start()

    def outer():
        g3.wait_recv()
        swap.wait_recv()

        def both(k):
            first = jnp.where(xh == 0, ao[k], aop[k])
            second = jnp.where(xh == 0, aop[k], ao[k])
            return jnp.concatenate([first, second], axis=1)

        anchor = both(0)
        delta = anchor - (s2[...] + r3[...]) / (2 * NZ * 2)
        new_momentum = outer_mu * both(1) + delta
        new_anchor = anchor - outer_rate * (delta + outer_mu * new_momentum)
        nm_ref[...] = jnp.where(xh == 0, new_momentum[:, :ROWS], new_momentum[:, ROWS:])
        na_ref[...] = jnp.where(xh == 0, new_anchor[:, :ROWS], new_anchor[:, ROWS:])
        mine[...] = new_anchor
        for copy in z4:
            copy.start()

    def share_core():
        for copy in z4:
            copy.wait_recv()
        g5.start()

    def make_ig_partner():
        for i in range(NPAIR):
            for k, rows in enumerate((pl.ds(0, SIDE // 2), pl.ds(PAIR - SIDE // 2, SIDE // 2))):
                igs[i, :, k * (SIDE // 2) : (k + 1) * (SIDE // 2)] = dot(cp[...], wf[i, rows], ((1,), (1,))).astype(BF16)
            send_ig[i].start()

    def make_ig_own():
        for i in range(NPAIR):
            ig_own[i] = dot(cm[...], wf[i], ((1,), (1,))).astype(BF16)
            ig_mid[i] = dot(cm[...], wo[i], ((1,), (1,))).astype(BF16)

    def finish():
        for load in loads[2:]:
            load.wait()
        g5.wait_recv()
        turned = fa[...].reshape(KV // 2, 2 * ROWS).T
        full_anchor = jnp.concatenate([turned[:ROWS], turned[ROWS:]], axis=1)
        for j in range(RS_SUBS):
            rows = pl.ds(j * rsub, rsub)
            for d in range(2):
                rs(d, 3, j).wait_recv()
            gradient = block(part, y, (j * rsub, rsub))[...] + rb[0, 2, rows].astype(F32) + rb[1, 2, rows].astype(F32)
            new_first = beta_one * m1[rows] + (1.0 - beta_one) * gradient
            new_second = beta_two * m2[rows] + (1.0 - beta_two) * gradient * gradient
            nf_ref[rows] = new_first
            ns_ref[rows] = new_second
            weights = block(wf, y, (j * rsub, rsub))[...].astype(F32)
            update = new_first / (jnp.sqrt(new_second) + adam_eps)
            inner = weights - learn_rate * (update + decay_rate * weights)
            blend = blend_keep * inner + (1.0 - blend_keep) * full_anchor[j * rsub : (j + 1) * rsub]
            nw_ref[rows] = blend.astype(BF16)

    send_mid.start()
    send_c.start()
    ag_forward(0)
    send_x[0].start()
    swap.start()
    transpose_weight()
    ag_forward(1)
    mid_forward(0)
    z_ready()
    send_x[1].start()
    ag_forward(2)
    make_part(0)
    rs_step(0)
    send_x[2].start()
    mid_forward(1)
    ag_forward(3)
    sum_z()
    make_part(1)
    sum_core()
    send_x[3].start()
    rs_step(1)
    mid_forward(2)
    outer()
    ag_forward(4)
    make_ig_partner()
    make_part(2)
    rs_step(2)
    mid_forward(3)
    make_part(3)
    rs_step(3)
    share_core()
    mid_forward(4)
    make_ig_own()
    finish()
    for copy in send_ig:
        copy.wait_recv()
    for copy in (send_mid, send_c, *send_x, *send_ig, *z1, g2, g3, *z4, g5, swap):
        copy.wait_send()
    for s in range(NY // 2):
        for d in range(2):
            mid(d, s).wait_send()
            for j in ag_subs(d, s):
                ag(d, s, j).wait_send()
            for j in range(RS_SUBS):
                rs(d, s, j).wait_send()


def write_kernel(half_ref, ig_own, ig_recv, ig_mid, nw, nf, ns, na, nm, o_ig, o_nw, o_nf, o_ns, o_na, o_nm, sem):
    half = half_ref[0]
    copies = []
    for i in range(NPAIR):
        for which, source, start, size in (
            (half, ig_own.at[i], 0, PAIR),
            (1 - half, ig_recv.at[i, :, pl.ds(0, SIDE // 2)], 0, SIDE // 2),
            (1 - half, ig_mid.at[i], SIDE // 2, MID),
            (1 - half, ig_recv.at[i, :, pl.ds(SIDE // 2, SIDE // 2)], SIDE // 2 + MID, SIDE // 2),
        ):
            columns = pl.ds(pl.multiple_of(which * (D // 2) + i * PAIR + start, 128), size)
            copies.append((source, o_ig.at[:, columns]))
    copies += [(nw, o_nw), (nf, o_nf), (ns, o_ns), (na, o_na), (nm, o_nm)]
    copies = [pltpu.make_async_copy(src, dst, sem.at[k]) for k, (src, dst) in enumerate(copies)]
    for copy in copies:
        copy.start()
    for copy in copies:
        copy.wait()


def body(layer_input, cotangent, local_weight, first_moment, second_moment, anchor, outer_momentum):
    vmem = pl.BlockSpec(memory_space=pltpu.VMEM)
    hbm = pl.BlockSpec(memory_space=pl.ANY)
    shape = jax.ShapeDtypeStruct
    dma = pltpu.SemaphoreType.DMA
    small = shape((SHARE, ROWS), F32)
    wide = shape((ROWS, KV), F32)
    results = pl.pallas_call(
        step_kernel,
        out_shape=(
            shape((NPAIR, TOK, PAIR), BF16), shape((NPAIR, TOK, SIDE), BF16), shape((NPAIR, TOK, MID), BF16),
            shape((ROWS, KV), BF16), wide, wide, small, small,
        ),
        in_specs=[hbm] * 7,
        out_specs=[vmem] * 8,
        scratch_shapes=[
            pltpu.VMEM((NPAIR, TOK, PAIR), BF16),
            pltpu.VMEM((NPAIR, TOK, PAIR), BF16),
            pltpu.VMEM((TOK, KV), BF16),
            pltpu.VMEM((TOK, KV), BF16),
            pltpu.VMEM((NPAIR, PAIR, KV), BF16),
            pltpu.VMEM((NPAIR, MID, KV), BF16),
            pltpu.VMEM((NPAIR, PAIR, KV), F32),
            pltpu.VMEM((2, ROWS, KV // 2), BF16),
            pltpu.VMEM((2, 3, ROWS, KV), BF16),
            pltpu.VMEM((2, ROWS, KV // 2), BF16),
            pltpu.VMEM((2, 3, ROWS, KV), BF16),
            pltpu.VMEM((NPAIR, TOK, SIDE), BF16),
            pltpu.VMEM((NZ, 2 * SHARE, 2 * ROWS), BF16),
            pltpu.VMEM((NZ - 1, 2 * SHARE, 2 * ROWS), BF16),
            pltpu.VMEM((2, SHARE, 2 * ROWS), F32),
            pltpu.VMEM((SHARE, 2 * ROWS), F32),
            pltpu.VMEM((SHARE, 2 * ROWS), F32),
            pltpu.VMEM((SHARE, 2 * ROWS), F32),
            pltpu.VMEM((2, SHARE, ROWS), F32),
            pltpu.VMEM((2, SHARE, ROWS), F32),
            pltpu.VMEM((NZ, 2, SHARE, 2 * ROWS), F32),
            pltpu.VMEM((ROWS, KV), F32),
            pltpu.VMEM((ROWS, KV), F32),
            dma((2 + NPAIR + 4,)),
            dma((2 + 2 * NPAIR,)), dma((2 + 2 * NPAIR,)),
            dma((2, NY // 2, AG_SUBS)), dma((2, NY // 2, AG_SUBS)),
            dma((2, NY // 2)), dma((2, NY // 2)),
            dma((2, NY // 2, RS_SUBS)), dma((2, NY // 2, RS_SUBS)),
            dma((NZ - 1,)), dma((NZ - 1,)),
            dma((NZ - 1,)), dma((NZ - 1,)),
            dma((4,)), dma((4,)),
            pltpu.SemaphoreType.REGULAR, pltpu.SemaphoreType.REGULAR,
        ],
        compiler_params=pltpu.CompilerParams(
            collective_id=0, has_side_effects=True, vmem_limit_bytes=40 << 20
        ),
        cost_estimate=pl.CostEstimate(flops=1_600_000_000, bytes_accessed=5_000_000, transcendentals=200_000),
        name="step",
    )(
        *(
            pltpu.with_memory_space_constraint(array, pltpu.HBM)
            for array in (
                layer_input, cotangent, local_weight[0], first_moment[0], second_moment[0], anchor.T, outer_momentum.T
            )
        )
    )
    half = (lax.axis_index("fsdp") // NY).astype(jnp.int32).reshape(1)
    outs = pl.pallas_call(
        write_kernel,
        out_shape=(shape((TOK, D), BF16), shape((ROWS, KV), BF16), wide, wide, small, small),
        in_specs=[pl.BlockSpec(memory_space=pltpu.SMEM)] + [vmem] * 8,
        out_specs=[hbm] * 6,
        scratch_shapes=[dma((4 * NPAIR + 5,))],
        name="write",
    )(half, *(pltpu.with_memory_space_constraint(array, pltpu.VMEM) for array in results))
    input_grad, new_weight, new_first, new_second, new_anchor, new_momentum = outs
    return input_grad, new_weight[None], new_first[None], new_second[None], new_anchor.T, new_momentum.T


def solution(mesh):
    in_specs = (
        P(("replica", "fsdp"), None),
        P(("replica", "fsdp"), None),
        P("replica", "fsdp", None),
        P("replica", "fsdp", None),
        P("replica", "fsdp", None),
        P("fsdp", "replica"),
        P("fsdp", "replica"),
    )
    out_specs = (
        P(("replica", "fsdp"), None),
        P("replica", "fsdp", None),
        P("replica", "fsdp", None),
        P("replica", "fsdp", None),
        P("fsdp", "replica"),
        P("fsdp", "replica"),
    )
    return jax.shard_map(body, mesh=mesh, in_specs=in_specs, out_specs=out_specs, check_vma=False)
```

```python
import jax
import jax.numpy as jnp
from jax import lax
from jax.experimental import pallas as pl
from jax.experimental.pallas import tpu as pltpu
from jax.sharding import PartitionSpec as P

beta_one = 0.9
beta_two = 0.95
adam_eps = 1e-08
learn_rate = 0.0003
decay_rate = 0.1
outer_rate = 0.7
outer_mu = 0.9
blend_keep = 0.5

MESH = pl.DeviceIdType.MESH
NY = 8
NZ = 8
TOK = 240
D = 3072
KV = 512
ROWS = 192
PAIR = 2 * ROWS
NPAIR = NY // 2
AG_SUBS = 2
RS_SUBS = 2
MID = 128
SIDE = PAIR - MID
X_PIECES = [(0, pl.ds(0, TOK)), (1, pl.ds(0, TOK)), (2, pl.ds(0, TOK)), (3, pl.ds(0, 128)), (3, pl.ds(128, TOK - 128))]
LATE = 4
SHARE = 16
F32 = jnp.float32
BF16 = jnp.bfloat16


def mod(value, size):
    return lax.rem(value + size, size)


def dot(a, b, dims):
    return lax.dot_general(a, b, (dims, ((), ())), preferred_element_type=F32)


def step_kernel(
    x_ref, c_ref, w_ref, m1_ref, m2_ref, a_ref, om_ref,
    ig_own, ig_recv, ig_mid, nw_ref, nf_ref, ns_ref, na_ref, nm_ref,
    xo, xp, cm, cp, wf, wo, part, sb0, sb, rb0, rb, igs, wt, r1, s1, r2, ao, aop, fa, m1, m2,
    local_sem, xs, xr, ag_s, ag_r, mid_s, mid_r, rs_s, rs_r, z1_s, z1_r, z4_s, z4_r, g_s, g_r, hello, ready,
):
    rep = lax.axis_index("replica")
    fs = lax.axis_index("fsdp")
    half, y = fs // NY, lax.rem(fs, NY)
    xh, z, core = rep // (NZ * 2), lax.rem(rep // 2, NZ), lax.rem(rep, 2)

    def rep_of(xh_, z_, core_):
        return (xh_ * NZ + z_) * 2 + core_

    partner = (rep, (1 - half) * NY + y)
    ring = ((rep, half * NY + mod(y + 1, NY)), (rep, half * NY + mod(y - 1, NY)))
    zs = [(rep_of(xh, mod(z + d, NZ), core), fs) for d in range(1, NZ)]
    twin = (rep_of(xh, z, 1 - core), fs)
    other = (rep_of(1 - xh, z, core), fs)
    cross = (rep_of(1 - xh, z, 1 - core), fs)
    near = (partner, *ring)
    far = (*zs, twin, other, cross)
    white = lax.rem(half + y, 2) == 0

    def signal(sem, peer):
        pl.semaphore_signal(sem, inc=1, device_id=peer, device_id_type=MESH)

    early, late = z < LATE, z >= LATE

    barrier = pltpu.get_barrier_semaphore()

    @pl.when(jnp.logical_not(white))
    def _():
        for peer in near:
            signal(barrier, peer)

    def remote(src, dst, send, recv, peer):
        return pltpu.make_async_remote_copy(src, dst, send, recv, device_id=peer, device_id_type=MESH)

    quad = y // 2
    odd = lax.rem(y, 2)
    order = [mod(quad + 2, NPAIR), mod(quad + 1 + 2 * odd, NPAIR), mod(quad + 3 + 2 * odd, NPAIR), quad]

    def pair_columns(which, pair):
        return pl.ds(pl.multiple_of(which * (D // 2) + pair * PAIR, 128), PAIR)

    def block(ref, b, rows):
        start = pl.multiple_of(lax.rem(b, 2) * ROWS + rows[0], 16)
        return ref.at[b // 2, pl.ds(start, rows[1])]

    load_w = pltpu.make_async_copy(w_ref, block(wf, y, (0, ROWS)), local_sem.at[0])
    load_c = pltpu.make_async_copy(c_ref, cm, local_sem.at[1])
    load_w.start()
    load_c.start()
    load_x = [
        pltpu.make_async_copy(x_ref.at[:, pair_columns(half, order[i])], xo.at[order[i]], local_sem.at[2 + i])
        for i in range(NPAIR)
    ]
    loads = [
        pltpu.make_async_copy(src, dst, local_sem.at[2 + NPAIR + i])
        for i, (src, dst) in enumerate(((a_ref, ao.at[0]), (om_ref, ao.at[1]), (m1_ref, m1), (m2_ref, m2)))
    ]
    for load in (*loads[:2], *load_x, *loads[2:]):
        load.start()
    load_w.wait()
    load_c.wait()

    @pl.when(white)
    def _():
        pl.semaphore_wait(barrier, len(near))
        for peer in near:
            signal(hello, peer)

    @pl.when(jnp.logical_not(white))
    def _():
        pl.semaphore_wait(hello, len(near))
        for peer in far:
            signal(barrier, peer)

    send_c = remote(cm, cp, xs.at[0], xr.at[0], partner)
    send_x = [
        remote(
            x_ref.at[rows, pair_columns(1 - half, order[i])], xp.at[order[i], rows], xs.at[1 + k], xr.at[1 + k], partner
        )
        for k, (i, rows) in enumerate(X_PIECES)
    ]
    send_ig = [
        remote(igs.at[i], ig_recv.at[i], xs.at[2 + NPAIR + i], xr.at[2 + NPAIR + i], partner) for i in range(NPAIR)
    ]

    sub = ROWS // AG_SUBS

    def ag(d, s, j):
        place = block(wf, mod(y - s, NY) if d == 0 else mod(y + s, NY), (j * sub, sub))
        return remote(place, place, ag_s.at[d, s, j], ag_r.at[d, s, j], ring[d])

    def ag_subs(d, s):
        if s < NY // 2 - 1:
            return range(AG_SUBS)
        return range(AG_SUBS // 2) if d == 0 else range(AG_SUBS // 2, AG_SUBS)

    def ag_forward(s, js=range(AG_SUBS)):
        for j in js:
            for d in range(2):
                if s > 0 and j in ag_subs(d, s - 1):
                    ag(d, s - 1, j).wait_recv()
                if s < NY // 2 and j in ag_subs(d, s):
                    ag(d, s, j).start()

    middle = pl.ds(pl.multiple_of(MID // 2 * odd, 16), MID // 2)
    send_mid = remote(
        wf.at[quad, pl.ds(pl.multiple_of(MID + MID // 2 * odd, 16), MID // 2)], wo.at[quad, middle],
        xs.at[2 + 2 * NPAIR], xr.at[2 + 2 * NPAIR], partner,
    )

    def mid(d, s):
        b = mod(y - s, NY) if d == 0 else mod(y + s, NY)
        start, size = (0, MID // 2) if s < NY // 2 - 1 else (d * (MID // 4), MID // 4)
        place = wo.at[b // 2, pl.ds(pl.multiple_of(lax.rem(b, 2) * (MID // 2) + start, 16), size)]
        return remote(place, place, mid_s.at[d, s], mid_r.at[d, s], ring[d])

    def mid_forward(s):
        if s == 0:
            send_mid.wait_recv()
        for d in range(2):
            if s > 0:
                mid(d, s - 1).wait_recv()
            if s < NY // 2:
                mid(d, s).start()

    rsub = ROWS // RS_SUBS

    def rs(d, s, j):
        rows = pl.ds(j * rsub, rsub)
        if s == 0:
            return remote(sb0.at[d, rows], rb0.at[d, rows], rs_s.at[d, s, j], rs_r.at[d, s, j], ring[d])
        return remote(sb.at[d, s - 1, rows], rb.at[d, s - 1, rows], rs_s.at[d, s, j], rs_r.at[d, s, j], ring[d])

    def rs_step(s, js=range(RS_SUBS)):
        for j in js:
            rows = pl.ds(j * rsub, rsub)
            for d in range(2):
                dest = mod(y + 4 - s, NY) if d == 0 else mod(y - 4 + s, NY)
                own = block(part, dest, (j * rsub, rsub))
                here = pl.ds(d * (KV // 2), KV // 2)
                there = pl.ds((1 - d) * (KV // 2), KV // 2)
                if s == 0:
                    sb0[d, rows] = own[:, here].astype(BF16)
                elif s == 1:
                    rs(d, 0, j).wait_recv()
                    sb[d, 0, rows, here] = (own[:, here] + rb0[d, rows].astype(F32)).astype(BF16)
                    sb[d, 0, rows, there] = own[:, there].astype(BF16)
                else:
                    rs(d, s - 1, j).wait_recv()
                    sb[d, s - 1, rows] = (own[...] + rb[d, s - 2, rows].astype(F32)).astype(BF16)
                rs(d, s, j).start()

    def make_part(i):
        if i == 0:
            send_c.wait_recv()
        load_x[i].wait()
        for copy, (pair, _) in zip(send_x, X_PIECES):
            if pair == i:
                copy.wait_recv()
        part[order[i]] = dot(xo[order[i]], cm[...], ((0,), (0,))) + dot(xp[order[i]], cp[...], ((0,), (0,)))

    z1 = [remote(wt.at[mod(z + d, NZ)], r1.at[d - 1], z1_s.at[d - 1], z1_r.at[d - 1], zs[d - 1]) for d in range(1, NZ)]
    g2 = [
        remote(s1.at[place], r2.at[k], g_s.at[k], g_r.at[k], peer)
        for k, (place, peer) in enumerate(((1 - core, twin), (core, other), (1 - core, cross)))
    ]
    mine = fa.at[z, core]
    z4 = [remote(mine, mine, z4_s.at[d], z4_r.at[d], zs[d]) for d in range(NZ - 1)]
    g5 = remote(fa.at[:, core], fa.at[:, core], g_s.at[3], g_r.at[3], twin)
    swap = remote(ao, aop, g_s.at[4], g_r.at[4], other)

    def transpose_weight():
        size = KV // 2
        eye = (
            lax.broadcasted_iota(jnp.int32, (size, size), 0) == lax.broadcasted_iota(jnp.int32, (size, size), 1)
        ).astype(BF16)
        own_w = block(wf, y, (0, ROWS))[...]
        stacked = jnp.concatenate([own_w[:, :size], own_w[:, size:]], axis=0)
        wt[...] = dot(eye, stacked, ((1,), (1,))).astype(BF16).reshape(NZ, 2 * SHARE, 2 * ROWS)

    def start_replica():
        @pl.when(jnp.logical_not(white))
        def _():
            pl.semaphore_wait(barrier, len(far))
            signal(ready, partner)

        @pl.when(white)
        def _():
            pl.semaphore_wait(ready, 1)

        for copy in z1:
            copy.start()
        for load in loads[:2]:
            load.wait()
        swap.start()

    def sum_z():
        for copy in z1:
            copy.wait_recv()
        total = wt[z].astype(F32)
        for d in range(NZ - 1):
            total = total + r1[d].astype(F32)
        s1[...] = total.reshape(2, SHARE, 2 * ROWS)
        for copy in g2:
            copy.start()

    def outer():
        for copy in (*g2, swap):
            copy.wait_recv()
        share = s1[core] + r2[0] + r2[1] + r2[2]

        def both(k):
            first = jnp.where(xh == 0, ao[k], aop[k])
            second = jnp.where(xh == 0, aop[k], ao[k])
            return jnp.concatenate([first, second], axis=1)

        anchor = both(0)
        delta = anchor - share / (2 * NZ * 2)
        new_momentum = outer_mu * both(1) + delta
        new_anchor = anchor - outer_rate * (delta + outer_mu * new_momentum)
        nm_ref[...] = jnp.where(xh == 0, new_momentum[:, :ROWS], new_momentum[:, ROWS:])
        na_ref[...] = jnp.where(xh == 0, new_anchor[:, :ROWS], new_anchor[:, ROWS:])
        mine[...] = new_anchor
        for copy in z4:
            copy.start()

    def share_core():
        for copy in z4:
            copy.wait_recv()
        g5.start()

    def make_ig_partner():
        for i in range(NPAIR):
            for k, rows in enumerate((pl.ds(0, SIDE // 2), pl.ds(PAIR - SIDE // 2, SIDE // 2))):
                igs[i, :, k * (SIDE // 2) : (k + 1) * (SIDE // 2)] = dot(cp[...], wf[i, rows], ((1,), (1,))).astype(BF16)
            send_ig[i].start()

    def make_ig_own():
        for i in range(NPAIR):
            ig_own[i] = dot(cm[...], wf[i], ((1,), (1,))).astype(BF16)
            ig_mid[i] = dot(cm[...], wo[i], ((1,), (1,))).astype(BF16)

    def finish():
        for load in loads[2:]:
            load.wait()
        g5.wait_recv()
        turned = fa[...].reshape(KV // 2, 2 * ROWS).T
        full_anchor = jnp.concatenate([turned[:ROWS], turned[ROWS:]], axis=1)
        for j in range(RS_SUBS):
            rows = pl.ds(j * rsub, rsub)
            for d in range(2):
                rs(d, 3, j).wait_recv()
            gradient = block(part, y, (j * rsub, rsub))[...] + rb[0, 2, rows].astype(F32) + rb[1, 2, rows].astype(F32)
            new_first = beta_one * m1[rows] + (1.0 - beta_one) * gradient
            new_second = beta_two * m2[rows] + (1.0 - beta_two) * gradient * gradient
            nf_ref[rows] = new_first
            ns_ref[rows] = new_second
            weights = block(wf, y, (j * rsub, rsub))[...].astype(F32)
            update = new_first / (jnp.sqrt(new_second) + adam_eps)
            inner = weights - learn_rate * (update + decay_rate * weights)
            blend = blend_keep * inner + (1.0 - blend_keep) * full_anchor[j * rsub : (j + 1) * rsub]
            nw_ref[rows] = blend.astype(BF16)

    send_mid.start()
    send_c.start()
    ag_forward(0)
    send_x[0].start()
    transpose_weight()
    pl.when(late)(start_replica)
    mid_forward(0)
    ag_forward(1)
    send_x[1].start()
    mid_forward(1)
    pl.when(early)(start_replica)
    ag_forward(2)
    make_part(0)
    rs_step(0)
    pl.when(late)(sum_z)
    send_x[2].start()
    ag_forward(3)
    make_part(1)
    send_x[3].start()
    rs_step(1)
    pl.when(early)(sum_z)
    send_x[4].start()
    pl.when(late)(outer)
    mid_forward(2)
    ag_forward(4)
    make_ig_partner()
    make_part(2)
    rs_step(2)
    pl.when(early)(outer)
    mid_forward(3)
    make_part(3)
    rs_step(3)
    share_core()
    mid_forward(4)
    make_ig_own()
    finish()
    for copy in send_ig:
        copy.wait_recv()
    for copy in (send_mid, send_c, *send_x, *send_ig, *z1, *g2, *z4, g5, swap):
        copy.wait_send()
    for s in range(NY // 2):
        for d in range(2):
            mid(d, s).wait_send()
            for j in ag_subs(d, s):
                ag(d, s, j).wait_send()
            for j in range(RS_SUBS):
                rs(d, s, j).wait_send()


def write_kernel(half_ref, ig_own, ig_recv, ig_mid, nw, nf, ns, na, nm, o_ig, o_nw, o_nf, o_ns, o_na, o_nm, sem):
    half = half_ref[0]
    copies = []
    for i in range(NPAIR):
        for which, source, start, size in (
            (half, ig_own.at[i], 0, PAIR),
            (1 - half, ig_recv.at[i, :, pl.ds(0, SIDE // 2)], 0, SIDE // 2),
            (1 - half, ig_mid.at[i], SIDE // 2, MID),
            (1 - half, ig_recv.at[i, :, pl.ds(SIDE // 2, SIDE // 2)], SIDE // 2 + MID, SIDE // 2),
        ):
            columns = pl.ds(pl.multiple_of(which * (D // 2) + i * PAIR + start, 128), size)
            copies.append((source, o_ig.at[:, columns]))
    copies += [(nw, o_nw), (nf, o_nf), (ns, o_ns), (na, o_na), (nm, o_nm)]
    copies = [pltpu.make_async_copy(src, dst, sem.at[k]) for k, (src, dst) in enumerate(copies)]
    for copy in copies:
        copy.start()
    for copy in copies:
        copy.wait()


def body(layer_input, cotangent, local_weight, first_moment, second_moment, anchor, outer_momentum):
    vmem = pl.BlockSpec(memory_space=pltpu.VMEM)
    hbm = pl.BlockSpec(memory_space=pl.ANY)
    shape = jax.ShapeDtypeStruct
    dma = pltpu.SemaphoreType.DMA
    small = shape((SHARE, ROWS), F32)
    wide = shape((ROWS, KV), F32)
    results = pl.pallas_call(
        step_kernel,
        out_shape=(
            shape((NPAIR, TOK, PAIR), BF16), shape((NPAIR, TOK, SIDE), BF16), shape((NPAIR, TOK, MID), BF16),
            shape((ROWS, KV), BF16), wide, wide, small, small,
        ),
        in_specs=[hbm] * 7,
        out_specs=[vmem] * 8,
        scratch_shapes=[
            pltpu.VMEM((NPAIR, TOK, PAIR), BF16),
            pltpu.VMEM((NPAIR, TOK, PAIR), BF16),
            pltpu.VMEM((TOK, KV), BF16),
            pltpu.VMEM((TOK, KV), BF16),
            pltpu.VMEM((NPAIR, PAIR, KV), BF16),
            pltpu.VMEM((NPAIR, MID, KV), BF16),
            pltpu.VMEM((NPAIR, PAIR, KV), F32),
            pltpu.VMEM((2, ROWS, KV // 2), BF16),
            pltpu.VMEM((2, 3, ROWS, KV), BF16),
            pltpu.VMEM((2, ROWS, KV // 2), BF16),
            pltpu.VMEM((2, 3, ROWS, KV), BF16),
            pltpu.VMEM((NPAIR, TOK, SIDE), BF16),
            pltpu.VMEM((NZ, 2 * SHARE, 2 * ROWS), BF16),
            pltpu.VMEM((NZ - 1, 2 * SHARE, 2 * ROWS), BF16),
            pltpu.VMEM((2, SHARE, 2 * ROWS), F32),
            pltpu.VMEM((3, SHARE, 2 * ROWS), F32),
            pltpu.VMEM((2, SHARE, ROWS), F32),
            pltpu.VMEM((2, SHARE, ROWS), F32),
            pltpu.VMEM((NZ, 2, SHARE, 2 * ROWS), F32),
            pltpu.VMEM((ROWS, KV), F32),
            pltpu.VMEM((ROWS, KV), F32),
            dma((2 + NPAIR + 4,)),
            dma((3 + 2 * NPAIR,)), dma((3 + 2 * NPAIR,)),
            dma((2, NY // 2, AG_SUBS)), dma((2, NY // 2, AG_SUBS)),
            dma((2, NY // 2)), dma((2, NY // 2)),
            dma((2, NY // 2, RS_SUBS)), dma((2, NY // 2, RS_SUBS)),
            dma((NZ - 1,)), dma((NZ - 1,)),
            dma((NZ - 1,)), dma((NZ - 1,)),
            dma((5,)), dma((5,)),
            pltpu.SemaphoreType.REGULAR, pltpu.SemaphoreType.REGULAR,
        ],
        compiler_params=pltpu.CompilerParams(
            collective_id=0, has_side_effects=True, vmem_limit_bytes=40 << 20
        ),
        cost_estimate=pl.CostEstimate(flops=1_600_000_000, bytes_accessed=5_000_000, transcendentals=200_000),
        name="step",
    )(
        *(
            pltpu.with_memory_space_constraint(array, pltpu.HBM)
            for array in (
                layer_input, cotangent, local_weight[0], first_moment[0], second_moment[0], anchor.T, outer_momentum.T
            )
        )
    )
    half = (lax.axis_index("fsdp") // NY).astype(jnp.int32).reshape(1)
    outs = pl.pallas_call(
        write_kernel,
        out_shape=(shape((TOK, D), BF16), shape((ROWS, KV), BF16), wide, wide, small, small),
        in_specs=[pl.BlockSpec(memory_space=pltpu.SMEM)] + [vmem] * 8,
        out_specs=[hbm] * 6,
        scratch_shapes=[dma((4 * NPAIR + 5,))],
        name="write",
    )(half, *(pltpu.with_memory_space_constraint(array, pltpu.VMEM) for array in results))
    input_grad, new_weight, new_first, new_second, new_anchor, new_momentum = outs
    return input_grad, new_weight[None], new_first[None], new_second[None], new_anchor.T, new_momentum.T


def solution(mesh):
    in_specs = (
        P(("replica", "fsdp"), None),
        P(("replica", "fsdp"), None),
        P("replica", "fsdp", None),
        P("replica", "fsdp", None),
        P("replica", "fsdp", None),
        P("fsdp", "replica"),
        P("fsdp", "replica"),
    )
    out_specs = (
        P(("replica", "fsdp"), None),
        P("replica", "fsdp", None),
        P("replica", "fsdp", None),
        P("replica", "fsdp", None),
        P("fsdp", "replica"),
        P("fsdp", "replica"),
    )
    return jax.shard_map(body, mesh=mesh, in_specs=in_specs, out_specs=out_specs, check_vma=False)
```

```python
import jax
import jax.numpy as jnp
from jax import lax
from jax.experimental import pallas as pl
from jax.experimental.pallas import tpu as pltpu
from jax.sharding import PartitionSpec as P

beta_one = 0.9
beta_two = 0.95
adam_eps = 1e-08
learn_rate = 0.0003
decay_rate = 0.1
outer_rate = 0.7
outer_mu = 0.9
blend_keep = 0.5

MESH = pl.DeviceIdType.MESH
NY = 8
NZ = 8
TOK = 240
D = 3072
KV = 512
ROWS = 192
PAIR = 2 * ROWS
NPAIR = NY // 2
AG_SUBS = 2
RS_SUBS = 2
MID = 128
SIDE = PAIR - MID
X_PIECES = [(0, pl.ds(0, TOK)), (1, pl.ds(0, TOK)), (2, pl.ds(0, TOK)), (3, pl.ds(0, 128)), (3, pl.ds(128, TOK - 128))]
LATE = 4
SHARE = 16
F32 = jnp.float32
BF16 = jnp.bfloat16


def mod(value, size):
    return lax.rem(value + size, size)


def dot(a, b, dims):
    return lax.dot_general(a, b, (dims, ((), ())), preferred_element_type=F32)


def step_kernel(
    x_ref, c_ref, w_ref, m1_ref, m2_ref, a_ref, om_ref,
    ig_own, ig_recv, ig_mid, nw_ref, nf_ref, ns_ref, na_ref, nm_ref,
    xo, xp, cm, cp, wf, wo, part, sb0, sb, rb0, rb, igs, wt, r1, s1, r2, ao, aop, fa, m1, m2,
    local_sem, xs, xr, ag_s, ag_r, mid_s, mid_r, rs_s, rs_r, z1_s, z1_r, z4_s, z4_r, g_s, g_r, hello, ready,
):
    rep = lax.axis_index("replica")
    fs = lax.axis_index("fsdp")
    half, y = fs // NY, lax.rem(fs, NY)
    xh, z, core = rep // (NZ * 2), lax.rem(rep // 2, NZ), lax.rem(rep, 2)

    def rep_of(xh_, z_, core_):
        return (xh_ * NZ + z_) * 2 + core_

    partner = (rep, (1 - half) * NY + y)
    ring = ((rep, half * NY + mod(y + 1, NY)), (rep, half * NY + mod(y - 1, NY)))
    zs = [(rep_of(xh, mod(z + d, NZ), core), fs) for d in range(1, NZ)]
    twin = (rep_of(xh, z, 1 - core), fs)
    other = (rep_of(1 - xh, z, core), fs)
    cross = (rep_of(1 - xh, z, 1 - core), fs)
    near = (partner, *ring)
    far = (*zs, twin, other, cross)
    white = lax.rem(half + y, 2) == 0

    def signal(sem, peer):
        pl.semaphore_signal(sem, inc=1, device_id=peer, device_id_type=MESH)

    late, first = z >= LATE, rep + fs == 0
    early = jnp.logical_not(jnp.logical_or(late, first))
    not_early = jnp.logical_or(late, first)

    barrier = pltpu.get_barrier_semaphore()

    @pl.when(jnp.logical_not(white))
    def _():
        for peer in near:
            signal(barrier, peer)

    def remote(src, dst, send, recv, peer):
        return pltpu.make_async_remote_copy(src, dst, send, recv, device_id=peer, device_id_type=MESH)

    quad = y // 2
    odd = lax.rem(y, 2)
    order = [mod(quad + 2, NPAIR), mod(quad + 1 + 2 * odd, NPAIR), mod(quad + 3 + 2 * odd, NPAIR), quad]

    def pair_columns(which, pair):
        return pl.ds(pl.multiple_of(which * (D // 2) + pair * PAIR, 128), PAIR)

    def block(ref, b, rows):
        start = pl.multiple_of(lax.rem(b, 2) * ROWS + rows[0], 16)
        return ref.at[b // 2, pl.ds(start, rows[1])]

    load_w = pltpu.make_async_copy(w_ref, block(wf, y, (0, ROWS)), local_sem.at[0])
    load_c = pltpu.make_async_copy(c_ref, cm, local_sem.at[1])
    load_w.start()
    load_c.start()
    load_x = [
        pltpu.make_async_copy(x_ref.at[:, pair_columns(half, order[i])], xo.at[order[i]], local_sem.at[2 + i])
        for i in range(NPAIR)
    ]
    loads = [
        pltpu.make_async_copy(src, dst, local_sem.at[2 + NPAIR + i])
        for i, (src, dst) in enumerate(((a_ref, ao.at[0]), (om_ref, ao.at[1]), (m1_ref, m1), (m2_ref, m2)))
    ]
    for load in (*loads[:2], *load_x, *loads[2:]):
        load.start()
    load_w.wait()
    load_c.wait()

    @pl.when(white)
    def _():
        pl.semaphore_wait(barrier, len(near))
        for peer in near:
            signal(hello, peer)

    @pl.when(jnp.logical_not(white))
    def _():
        pl.semaphore_wait(hello, len(near))
        for peer in far:
            signal(barrier, peer)

    send_c = remote(cm, cp, xs.at[0], xr.at[0], partner)
    send_x = [
        remote(
            x_ref.at[rows, pair_columns(1 - half, order[i])], xp.at[order[i], rows], xs.at[1 + k], xr.at[1 + k], partner
        )
        for k, (i, rows) in enumerate(X_PIECES)
    ]
    send_ig = [
        remote(igs.at[i], ig_recv.at[i], xs.at[2 + NPAIR + i], xr.at[2 + NPAIR + i], partner) for i in range(NPAIR)
    ]

    sub = ROWS // AG_SUBS

    def ag(d, s, j):
        place = block(wf, mod(y - s, NY) if d == 0 else mod(y + s, NY), (j * sub, sub))
        return remote(place, place, ag_s.at[d, s, j], ag_r.at[d, s, j], ring[d])

    def ag_subs(d, s):
        if s < NY // 2 - 1:
            return range(AG_SUBS)
        return range(AG_SUBS // 2) if d == 0 else range(AG_SUBS // 2, AG_SUBS)

    def ag_forward(s, js=range(AG_SUBS)):
        for j in js:
            for d in range(2):
                if s > 0 and j in ag_subs(d, s - 1):
                    ag(d, s - 1, j).wait_recv()
                if s < NY // 2 and j in ag_subs(d, s):
                    ag(d, s, j).start()

    middle = pl.ds(pl.multiple_of(MID // 2 * odd, 16), MID // 2)
    send_mid = remote(
        wf.at[quad, pl.ds(pl.multiple_of(MID + MID // 2 * odd, 16), MID // 2)], wo.at[quad, middle],
        xs.at[2 + 2 * NPAIR], xr.at[2 + 2 * NPAIR], partner,
    )

    def mid(d, s):
        b = mod(y - s, NY) if d == 0 else mod(y + s, NY)
        start, size = (0, MID // 2) if s < NY // 2 - 1 else (d * (MID // 4), MID // 4)
        place = wo.at[b // 2, pl.ds(pl.multiple_of(lax.rem(b, 2) * (MID // 2) + start, 16), size)]
        return remote(place, place, mid_s.at[d, s], mid_r.at[d, s], ring[d])

    def mid_forward(s):
        if s == 0:
            send_mid.wait_recv()
        for d in range(2):
            if s > 0:
                mid(d, s - 1).wait_recv()
            if s < NY // 2:
                mid(d, s).start()

    rsub = ROWS // RS_SUBS

    def rs(d, s, j):
        rows = pl.ds(j * rsub, rsub)
        if s == 0:
            return remote(sb0.at[d, rows], rb0.at[d, rows], rs_s.at[d, s, j], rs_r.at[d, s, j], ring[d])
        return remote(sb.at[d, s - 1, rows], rb.at[d, s - 1, rows], rs_s.at[d, s, j], rs_r.at[d, s, j], ring[d])

    def rs_step(s, js=range(RS_SUBS)):
        for j in js:
            rows = pl.ds(j * rsub, rsub)
            for d in range(2):
                dest = mod(y + 4 - s, NY) if d == 0 else mod(y - 4 + s, NY)
                own = block(part, dest, (j * rsub, rsub))
                here = pl.ds(d * (KV // 2), KV // 2)
                there = pl.ds((1 - d) * (KV // 2), KV // 2)
                if s == 0:
                    sb0[d, rows] = own[:, here].astype(BF16)
                elif s == 1:
                    rs(d, 0, j).wait_recv()
                    sb[d, 0, rows, here] = (own[:, here] + rb0[d, rows].astype(F32)).astype(BF16)
                    sb[d, 0, rows, there] = own[:, there].astype(BF16)
                else:
                    rs(d, s - 1, j).wait_recv()
                    sb[d, s - 1, rows] = (own[...] + rb[d, s - 2, rows].astype(F32)).astype(BF16)
                rs(d, s, j).start()

    def make_part(i):
        if i == 0:
            send_c.wait_recv()
        load_x[i].wait()
        for copy, (pair, _) in zip(send_x, X_PIECES):
            if pair == i:
                copy.wait_recv()
        part[order[i]] = dot(xo[order[i]], cm[...], ((0,), (0,))) + dot(xp[order[i]], cp[...], ((0,), (0,)))

    z1 = [remote(wt.at[mod(z + d, NZ)], r1.at[d - 1], z1_s.at[d - 1], z1_r.at[d - 1], zs[d - 1]) for d in range(1, NZ)]
    g2 = [
        remote(s1.at[place], r2.at[k], g_s.at[k], g_r.at[k], peer)
        for k, (place, peer) in enumerate(((1 - core, twin), (core, other), (1 - core, cross)))
    ]
    mine = fa.at[z, core]
    z4 = [remote(mine, mine, z4_s.at[d], z4_r.at[d], zs[d]) for d in range(NZ - 1)]
    g5 = remote(fa.at[:, core], fa.at[:, core], g_s.at[3], g_r.at[3], twin)
    swap = remote(ao, aop, g_s.at[4], g_r.at[4], other)

    def transpose_weight():
        size = KV // 2
        eye = (
            lax.broadcasted_iota(jnp.int32, (size, size), 0) == lax.broadcasted_iota(jnp.int32, (size, size), 1)
        ).astype(BF16)
        own_w = block(wf, y, (0, ROWS))[...]
        stacked = jnp.concatenate([own_w[:, :size], own_w[:, size:]], axis=0)
        wt[...] = dot(eye, stacked, ((1,), (1,))).astype(BF16).reshape(NZ, 2 * SHARE, 2 * ROWS)

    def start_replica():
        @pl.when(jnp.logical_not(white))
        def _():
            pl.semaphore_wait(barrier, len(far))
            signal(ready, partner)

        @pl.when(white)
        def _():
            pl.semaphore_wait(ready, 1)

        for copy in z1:
            copy.start()
        for load in loads[:2]:
            load.wait()
        swap.start()

    def sum_z():
        for copy in z1:
            copy.wait_recv()
        total = wt[z].astype(F32)
        for d in range(NZ - 1):
            total = total + r1[d].astype(F32)
        s1[...] = total.reshape(2, SHARE, 2 * ROWS)
        for copy in g2:
            copy.start()

    def outer():
        for copy in (*g2, swap):
            copy.wait_recv()
        share = s1[core] + r2[0] + r2[1] + r2[2]

        def both(k):
            first = jnp.where(xh == 0, ao[k], aop[k])
            second = jnp.where(xh == 0, aop[k], ao[k])
            return jnp.concatenate([first, second], axis=1)

        anchor = both(0)
        delta = anchor - share / (2 * NZ * 2)
        new_momentum = outer_mu * both(1) + delta
        new_anchor = anchor - outer_rate * (delta + outer_mu * new_momentum)
        nm_ref[...] = jnp.where(xh == 0, new_momentum[:, :ROWS], new_momentum[:, ROWS:])
        na_ref[...] = jnp.where(xh == 0, new_anchor[:, :ROWS], new_anchor[:, ROWS:])
        mine[...] = new_anchor
        for copy in z4:
            copy.start()

    def share_core():
        for copy in z4:
            copy.wait_recv()
        g5.start()

    def make_ig_partner():
        for i in range(NPAIR):
            for k, rows in enumerate((pl.ds(0, SIDE // 2), pl.ds(PAIR - SIDE // 2, SIDE // 2))):
                igs[i, :, k * (SIDE // 2) : (k + 1) * (SIDE // 2)] = dot(cp[...], wf[i, rows], ((1,), (1,))).astype(BF16)
            send_ig[i].start()

    def make_ig_own():
        for i in range(NPAIR):
            ig_own[i] = dot(cm[...], wf[i], ((1,), (1,))).astype(BF16)
            ig_mid[i] = dot(cm[...], wo[i], ((1,), (1,))).astype(BF16)

    def finish():
        for load in loads[2:]:
            load.wait()
        g5.wait_recv()
        turned = fa[...].reshape(KV // 2, 2 * ROWS).T
        full_anchor = jnp.concatenate([turned[:ROWS], turned[ROWS:]], axis=1)
        for j in range(RS_SUBS):
            rows = pl.ds(j * rsub, rsub)
            for d in range(2):
                rs(d, 3, j).wait_recv()
            gradient = block(part, y, (j * rsub, rsub))[...] + rb[0, 2, rows].astype(F32) + rb[1, 2, rows].astype(F32)
            new_first = beta_one * m1[rows] + (1.0 - beta_one) * gradient
            new_second = beta_two * m2[rows] + (1.0 - beta_two) * gradient * gradient
            nf_ref[rows] = new_first
            ns_ref[rows] = new_second
            weights = block(wf, y, (j * rsub, rsub))[...].astype(F32)
            update = new_first / (jnp.sqrt(new_second) + adam_eps)
            inner = weights - learn_rate * (update + decay_rate * weights)
            blend = blend_keep * inner + (1.0 - blend_keep) * full_anchor[j * rsub : (j + 1) * rsub]
            nw_ref[rows] = blend.astype(BF16)

    send_mid.start()
    send_c.start()
    ag_forward(0)
    send_x[0].start()
    send_x[1].start()
    transpose_weight()
    pl.when(late)(start_replica)
    mid_forward(0)
    ag_forward(1)
    pl.when(first)(start_replica)
    mid_forward(1)
    pl.when(early)(start_replica)
    ag_forward(2)
    make_part(0)
    rs_step(0)
    pl.when(not_early)(sum_z)
    send_x[2].start()
    ag_forward(3)
    make_part(1)
    send_x[3].start()
    rs_step(1)
    pl.when(early)(sum_z)
    send_x[4].start()
    pl.when(not_early)(outer)
    mid_forward(2)
    ag_forward(4)
    make_ig_partner()
    make_part(2)
    rs_step(2)
    pl.when(early)(outer)
    mid_forward(3)
    make_part(3)
    rs_step(3)
    share_core()
    mid_forward(4)
    make_ig_own()
    for copy in (send_mid, send_c, *send_x, *z1, *g2, swap):
        copy.wait_send()
    for s in range(NY // 2):
        for d in range(2):
            mid(d, s).wait_send()
            for j in ag_subs(d, s):
                ag(d, s, j).wait_send()
            for j in range(RS_SUBS if s < NY // 2 - 1 else 0):
                rs(d, s, j).wait_send()
    finish()
    for copy in send_ig:
        copy.wait_recv()
    for copy in (*send_ig, *z4, g5):
        copy.wait_send()
    for d in range(2):
        for j in range(RS_SUBS):
            rs(d, NY // 2 - 1, j).wait_send()


def write_kernel(half_ref, ig_own, ig_recv, ig_mid, nw, nf, ns, na, nm, o_ig, o_nw, o_nf, o_ns, o_na, o_nm, sem):
    half = half_ref[0]
    copies = []
    for i in range(NPAIR):
        for which, source, start, size in (
            (half, ig_own.at[i], 0, PAIR),
            (1 - half, ig_recv.at[i, :, pl.ds(0, SIDE // 2)], 0, SIDE // 2),
            (1 - half, ig_mid.at[i], SIDE // 2, MID),
            (1 - half, ig_recv.at[i, :, pl.ds(SIDE // 2, SIDE // 2)], SIDE // 2 + MID, SIDE // 2),
        ):
            columns = pl.ds(pl.multiple_of(which * (D // 2) + i * PAIR + start, 128), size)
            copies.append((source, o_ig.at[:, columns]))
    copies += [(nw, o_nw), (nf, o_nf), (ns, o_ns), (na, o_na), (nm, o_nm)]
    copies = [pltpu.make_async_copy(src, dst, sem.at[k]) for k, (src, dst) in enumerate(copies)]
    for copy in copies:
        copy.start()
    for copy in copies:
        copy.wait()


def body(layer_input, cotangent, local_weight, first_moment, second_moment, anchor, outer_momentum):
    vmem = pl.BlockSpec(memory_space=pltpu.VMEM)
    hbm = pl.BlockSpec(memory_space=pl.ANY)
    shape = jax.ShapeDtypeStruct
    dma = pltpu.SemaphoreType.DMA
    small = shape((SHARE, ROWS), F32)
    wide = shape((ROWS, KV), F32)
    results = pl.pallas_call(
        step_kernel,
        out_shape=(
            shape((NPAIR, TOK, PAIR), BF16), shape((NPAIR, TOK, SIDE), BF16), shape((NPAIR, TOK, MID), BF16),
            shape((ROWS, KV), BF16), wide, wide, small, small,
        ),
        in_specs=[hbm] * 7,
        out_specs=[vmem] * 8,
        scratch_shapes=[
            pltpu.VMEM((NPAIR, TOK, PAIR), BF16),
            pltpu.VMEM((NPAIR, TOK, PAIR), BF16),
            pltpu.VMEM((TOK, KV), BF16),
            pltpu.VMEM((TOK, KV), BF16),
            pltpu.VMEM((NPAIR, PAIR, KV), BF16),
            pltpu.VMEM((NPAIR, MID, KV), BF16),
            pltpu.VMEM((NPAIR, PAIR, KV), F32),
            pltpu.VMEM((2, ROWS, KV // 2), BF16),
            pltpu.VMEM((2, 3, ROWS, KV), BF16),
            pltpu.VMEM((2, ROWS, KV // 2), BF16),
            pltpu.VMEM((2, 3, ROWS, KV), BF16),
            pltpu.VMEM((NPAIR, TOK, SIDE), BF16),
            pltpu.VMEM((NZ, 2 * SHARE, 2 * ROWS), BF16),
            pltpu.VMEM((NZ - 1, 2 * SHARE, 2 * ROWS), BF16),
            pltpu.VMEM((2, SHARE, 2 * ROWS), F32),
            pltpu.VMEM((3, SHARE, 2 * ROWS), F32),
            pltpu.VMEM((2, SHARE, ROWS), F32),
            pltpu.VMEM((2, SHARE, ROWS), F32),
            pltpu.VMEM((NZ, 2, SHARE, 2 * ROWS), F32),
            pltpu.VMEM((ROWS, KV), F32),
            pltpu.VMEM((ROWS, KV), F32),
            dma((2 + NPAIR + 4,)),
            dma((3 + 2 * NPAIR,)), dma((3 + 2 * NPAIR,)),
            dma((2, NY // 2, AG_SUBS)), dma((2, NY // 2, AG_SUBS)),
            dma((2, NY // 2)), dma((2, NY // 2)),
            dma((2, NY // 2, RS_SUBS)), dma((2, NY // 2, RS_SUBS)),
            dma((NZ - 1,)), dma((NZ - 1,)),
            dma((NZ - 1,)), dma((NZ - 1,)),
            dma((5,)), dma((5,)),
            pltpu.SemaphoreType.REGULAR, pltpu.SemaphoreType.REGULAR,
        ],
        compiler_params=pltpu.CompilerParams(
            collective_id=0, has_side_effects=True, vmem_limit_bytes=40 << 20
        ),
        cost_estimate=pl.CostEstimate(flops=1_600_000_000, bytes_accessed=5_000_000, transcendentals=200_000),
        name="step",
    )(
        *(
            pltpu.with_memory_space_constraint(array, pltpu.HBM)
            for array in (
                layer_input, cotangent, local_weight[0], first_moment[0], second_moment[0], anchor.T, outer_momentum.T
            )
        )
    )
    half = (lax.axis_index("fsdp") // NY).astype(jnp.int32).reshape(1)
    outs = pl.pallas_call(
        write_kernel,
        out_shape=(shape((TOK, D), BF16), shape((ROWS, KV), BF16), wide, wide, small, small),
        in_specs=[pl.BlockSpec(memory_space=pltpu.SMEM)] + [vmem] * 8,
        out_specs=[hbm] * 6,
        scratch_shapes=[dma((4 * NPAIR + 5,))],
        name="write",
    )(half, *(pltpu.with_memory_space_constraint(array, pltpu.VMEM) for array in results))
    input_grad, new_weight, new_first, new_second, new_anchor, new_momentum = outs
    return input_grad, new_weight[None], new_first[None], new_second[None], new_anchor.T, new_momentum.T


def solution(mesh):
    in_specs = (
        P(("replica", "fsdp"), None),
        P(("replica", "fsdp"), None),
        P("replica", "fsdp", None),
        P("replica", "fsdp", None),
        P("replica", "fsdp", None),
        P("fsdp", "replica"),
        P("fsdp", "replica"),
    )
    out_specs = (
        P(("replica", "fsdp"), None),
        P("replica", "fsdp", None),
        P("replica", "fsdp", None),
        P("replica", "fsdp", None),
        P("fsdp", "replica"),
        P("fsdp", "replica"),
    )
    return jax.shard_map(body, mesh=mesh, in_specs=in_specs, out_specs=out_specs, check_vma=False)
```

```python
import jax
import jax.numpy as jnp
from jax import lax
from jax.experimental import pallas as pl
from jax.experimental.pallas import tpu as pltpu
from jax.sharding import PartitionSpec as P

beta_one = 0.9
beta_two = 0.95
adam_eps = 1e-08
learn_rate = 0.0003
decay_rate = 0.1
outer_rate = 0.7
outer_mu = 0.9
blend_keep = 0.5

MESH = pl.DeviceIdType.MESH
NY = 8
NZ = 8
TOK = 240
D = 3072
KV = 512
ROWS = 192
PAIR = 2 * ROWS
NPAIR = NY // 2
AG_SUBS = 2
RS_SUBS = 2
MID = 128
SIDE = PAIR - MID
X_PIECES = [(0, pl.ds(0, TOK)), (1, pl.ds(0, TOK)), (2, pl.ds(0, TOK)), (3, pl.ds(0, 128)), (3, pl.ds(128, TOK - 128))]
LATE = 4
SHARE = 16
F32 = jnp.float32
BF16 = jnp.bfloat16


def mod(value, size):
    return lax.rem(value + size, size)


def dot(a, b, dims):
    return lax.dot_general(a, b, (dims, ((), ())), preferred_element_type=F32)


def step_kernel(
    x_ref, c_ref, w_ref, m1_ref, m2_ref, a_ref, om_ref,
    ig_own, ig_recv, ig_mid, nw_ref, nf_ref, ns_ref, na_ref, nm_ref,
    xo, xp, cm, cp, wf, wo, part, sb0, sb, rb0, rb, igs, igm, wt, r1, s1, r2, ao, fixed, fa, m1, m2,
    local_sem, xs, xr, ag_s, ag_r, mid_s, mid_r, rs_s, rs_r, z1_s, z1_r, z4_s, z4_r, g_s, g_r, hello, ready,
):
    rep = lax.axis_index("replica")
    fs = lax.axis_index("fsdp")
    half, y = fs // NY, lax.rem(fs, NY)
    xh, z, core = rep // (NZ * 2), lax.rem(rep // 2, NZ), lax.rem(rep, 2)

    def rep_of(xh_, z_, core_):
        return (xh_ * NZ + z_) * 2 + core_

    partner = (rep, (1 - half) * NY + y)
    ring = ((rep, half * NY + mod(y + 1, NY)), (rep, half * NY + mod(y - 1, NY)))
    zs = [(rep_of(xh, mod(z + d, NZ), core), fs) for d in range(1, NZ)]
    twin = (rep_of(xh, z, 1 - core), fs)
    other = (rep_of(1 - xh, z, core), fs)
    cross = (rep_of(1 - xh, z, 1 - core), fs)
    near = (partner, *ring)
    far = (*zs, twin, other, cross)
    white = lax.rem(half + y, 2) == 0

    def signal(sem, peer):
        pl.semaphore_signal(sem, inc=1, device_id=peer, device_id_type=MESH)

    late, first = z >= LATE, rep + fs == 0
    early = jnp.logical_not(jnp.logical_or(late, first))
    not_early = jnp.logical_or(late, first)

    barrier = pltpu.get_barrier_semaphore()

    @pl.when(jnp.logical_not(white))
    def _():
        for peer in near:
            signal(barrier, peer)

    def remote(src, dst, send, recv, peer):
        return pltpu.make_async_remote_copy(src, dst, send, recv, device_id=peer, device_id_type=MESH)

    quad = y // 2
    odd = lax.rem(y, 2)
    order = [mod(quad + 2, NPAIR), mod(quad + 1 + 2 * odd, NPAIR), mod(quad + 3 + 2 * odd, NPAIR), quad]

    def pair_columns(which, pair):
        return pl.ds(pl.multiple_of(which * (D // 2) + pair * PAIR, 128), PAIR)

    def block(ref, b, rows):
        start = pl.multiple_of(lax.rem(b, 2) * ROWS + rows[0], 16)
        return ref.at[b // 2, pl.ds(start, rows[1])]

    load_w = pltpu.make_async_copy(w_ref, block(wf, y, (0, ROWS)), local_sem.at[0])
    load_c = pltpu.make_async_copy(c_ref, cm, local_sem.at[1])
    load_w.start()
    load_c.start()
    load_x = [
        pltpu.make_async_copy(x_ref.at[:, pair_columns(half, order[i])], xo.at[order[i]], local_sem.at[2 + i])
        for i in range(NPAIR)
    ]
    loads = [
        pltpu.make_async_copy(src, dst, local_sem.at[2 + NPAIR + i])
        for i, (src, dst) in enumerate(((a_ref, ao.at[0]), (om_ref, ao.at[1]), (m1_ref, m1), (m2_ref, m2)))
    ]
    for load in (*loads[:2], *load_x, *loads[2:]):
        load.start()
    load_w.wait()
    load_c.wait()

    @pl.when(white)
    def _():
        pl.semaphore_wait(barrier, len(near))
        for peer in near:
            signal(hello, peer)

    @pl.when(jnp.logical_not(white))
    def _():
        pl.semaphore_wait(hello, len(near))
        for peer in far:
            signal(barrier, peer)

    send_c = remote(cm, cp, xs.at[0], xr.at[0], partner)
    send_x = [
        remote(
            x_ref.at[rows, pair_columns(1 - half, order[i])], xp.at[order[i], rows], xs.at[1 + k], xr.at[1 + k], partner
        )
        for k, (i, rows) in enumerate(X_PIECES)
    ]
    send_ig = [
        remote(igs.at[i], ig_recv.at[i], xs.at[2 + NPAIR + i], xr.at[2 + NPAIR + i], partner) for i in range(NPAIR)
    ]
    send_ig.append(remote(igm, ig_mid.at[order[0]], xs.at[3 + 2 * NPAIR], xr.at[3 + 2 * NPAIR], partner))

    sub = ROWS // AG_SUBS

    def ag(d, s, j):
        place = block(wf, mod(y - s, NY) if d == 0 else mod(y + s, NY), (j * sub, sub))
        return remote(place, place, ag_s.at[d, s, j], ag_r.at[d, s, j], ring[d])

    def ag_subs(d, s):
        if s < NY // 2 - 1:
            return range(AG_SUBS)
        return range(AG_SUBS // 2) if d == 0 else range(AG_SUBS // 2, AG_SUBS)

    def ag_forward(s, js=range(AG_SUBS)):
        for j in js:
            for d in range(2):
                if s > 0 and j in ag_subs(d, s - 1):
                    ag(d, s - 1, j).wait_recv()
                if s < NY // 2 and j in ag_subs(d, s):
                    ag(d, s, j).start()

    middle = pl.ds(pl.multiple_of(MID // 2 * odd, 16), MID // 2)
    send_mid = remote(
        wf.at[quad, pl.ds(pl.multiple_of(MID + MID // 2 * odd, 16), MID // 2)], wo.at[quad, middle],
        xs.at[2 + 2 * NPAIR], xr.at[2 + 2 * NPAIR], partner,
    )

    def mid(d, s):
        b = mod(y - s, NY) if d == 0 else mod(y + s, NY)
        place = wo.at[b // 2, pl.ds(pl.multiple_of(lax.rem(b, 2) * (MID // 2), 16), MID // 2)]
        return remote(place, place, mid_s.at[d, s], mid_r.at[d, s], ring[d])

    def mid_forward(s):
        if s == 0:
            send_mid.wait_recv()
        for d in range(2):
            if s in (1, 2):
                mid(d, s - 1).wait_recv()
            elif s == 3:
                pl.when(odd == 1 - d)(mid(d, 2).wait_recv)
            if s < 2:
                mid(d, s).start()
            elif s == 2:
                pl.when(odd == d)(mid(d, 2).start)

    rsub = ROWS // RS_SUBS

    def rs(d, s, j):
        rows = pl.ds(j * rsub, rsub)
        if s == 0:
            return remote(sb0.at[d, rows], rb0.at[d, rows], rs_s.at[d, s, j], rs_r.at[d, s, j], ring[d])
        return remote(sb.at[d, s - 1, rows], rb.at[d, s - 1, rows], rs_s.at[d, s, j], rs_r.at[d, s, j], ring[d])

    def rs_step(s, js=range(RS_SUBS)):
        for j in js:
            rows = pl.ds(j * rsub, rsub)
            for d in range(2):
                dest = mod(y + 4 - s, NY) if d == 0 else mod(y - 4 + s, NY)
                own = block(part, dest, (j * rsub, rsub))
                here = pl.ds(d * (KV // 2), KV // 2)
                there = pl.ds((1 - d) * (KV // 2), KV // 2)
                if s == 0:
                    sb0[d, rows] = own[:, here].astype(BF16)
                elif s == 1:
                    rs(d, 0, j).wait_recv()
                    sb[d, 0, rows, here] = (own[:, here] + rb0[d, rows].astype(F32)).astype(BF16)
                    sb[d, 0, rows, there] = own[:, there].astype(BF16)
                else:
                    rs(d, s - 1, j).wait_recv()
                    sb[d, s - 1, rows] = (own[...] + rb[d, s - 2, rows].astype(F32)).astype(BF16)
                rs(d, s, j).start()

    def make_part(i):
        if i == 0:
            send_c.wait_recv()
        load_x[i].wait()
        for copy, (pair, _) in zip(send_x, X_PIECES):
            if pair == i:
                copy.wait_recv()
        part[order[i]] = dot(xo[order[i]], cm[...], ((0,), (0,))) + dot(xp[order[i]], cp[...], ((0,), (0,)))

    z1 = [remote(wt.at[mod(z + d, NZ)], r1.at[d - 1], z1_s.at[d - 1], z1_r.at[d - 1], zs[d - 1]) for d in range(1, NZ)]
    g2 = [
        remote(s1.at[place], r2.at[k], g_s.at[k], g_r.at[k], peer)
        for k, (place, peer) in enumerate(((1 - core, twin), (core, other), (1 - core, cross)))
    ]
    mine = fa.at[z, core]
    z4 = [remote(mine, mine, z4_s.at[d], z4_r.at[d], zs[d]) for d in range(NZ - 1)]
    g5 = remote(fa.at[:, core], fa.at[:, core], g_s.at[3], g_r.at[3], twin)
    swap = remote(fixed.at[0], fixed.at[1], g_s.at[4], g_r.at[4], other)

    def transpose_weight():
        size = KV // 2
        eye = (
            lax.broadcasted_iota(jnp.int32, (size, size), 0) == lax.broadcasted_iota(jnp.int32, (size, size), 1)
        ).astype(BF16)
        own_w = block(wf, y, (0, ROWS))[...]
        stacked = jnp.concatenate([own_w[:, :size], own_w[:, size:]], axis=0)
        wt[...] = dot(eye, stacked, ((1,), (1,))).astype(BF16).reshape(NZ, 2 * SHARE, 2 * ROWS)

    def start_replica():
        @pl.when(jnp.logical_not(white))
        def _():
            pl.semaphore_wait(barrier, len(far))
            signal(ready, partner)

        @pl.when(white)
        def _():
            pl.semaphore_wait(ready, 1)

        for copy in z1:
            copy.start()
        for load in loads[:2]:
            load.wait()
        fixed[0] = ao[0] - outer_rate * ((1.0 + outer_mu) * ao[0] + outer_mu * outer_mu * ao[1])
        swap.start()

    def sum_z():
        for copy in z1:
            copy.wait_recv()
        total = wt[z].astype(F32)
        for d in range(NZ - 1):
            total = total + r1[d].astype(F32)
        s1[...] = total.reshape(2, SHARE, 2 * ROWS)
        for copy in g2:
            copy.start()

    def outer():
        for copy in (*g2, swap):
            copy.wait_recv()
        share = s1[core] + r2[0] + r2[1] + r2[2]

        mean = share / (2 * NZ * 2)
        mean_own = jnp.where(xh == 0, mean[:, :ROWS], mean[:, ROWS:])
        delta = ao[0] - mean_own
        new_momentum = outer_mu * ao[1] + delta
        own_anchor = ao[0] - outer_rate * (delta + outer_mu * new_momentum)
        nm_ref[...] = new_momentum
        na_ref[...] = own_anchor
        mean_other = jnp.where(xh == 0, mean[:, ROWS:], mean[:, :ROWS])
        other_anchor = fixed[1] + (outer_rate * (1.0 + outer_mu)) * mean_other
        first = jnp.where(xh == 0, own_anchor, other_anchor)
        second = jnp.where(xh == 0, other_anchor, own_anchor)
        new_anchor = jnp.concatenate([first, second], axis=1)
        mine[...] = new_anchor
        for copy in z4:
            copy.start()

    def share_core():
        for copy in z4:
            copy.wait_recv()
        g5.start()

    def make_ig_partner():
        for i in range(NPAIR):
            for k, rows in enumerate((pl.ds(0, SIDE // 2), pl.ds(PAIR - SIDE // 2, SIDE // 2))):
                igs[i, :, k * (SIDE // 2) : (k + 1) * (SIDE // 2)] = dot(cp[...], wf[i, rows], ((1,), (1,))).astype(BF16)
            send_ig[i].start()
        igm[...] = dot(cp[...], wf[order[0], pl.ds(SIDE // 2, MID)], ((1,), (1,))).astype(BF16)
        send_ig[NPAIR].start()

    def make_ig_own():
        for i in range(NPAIR):
            ig_own[i] = dot(cm[...], wf[i], ((1,), (1,))).astype(BF16)
        for i in range(1, NPAIR):
            ig_mid[order[i]] = dot(cm[...], wo[order[i]], ((1,), (1,))).astype(BF16)

    def finish():
        for load in loads[2:]:
            load.wait()
        g5.wait_recv()
        turned = fa[...].reshape(KV // 2, 2 * ROWS).T
        full_anchor = jnp.concatenate([turned[:ROWS], turned[ROWS:]], axis=1)
        for j in range(RS_SUBS):
            rows = pl.ds(j * rsub, rsub)
            for d in range(2):
                rs(d, 3, j).wait_recv()
            gradient = block(part, y, (j * rsub, rsub))[...] + rb[0, 2, rows].astype(F32) + rb[1, 2, rows].astype(F32)
            new_first = beta_one * m1[rows] + (1.0 - beta_one) * gradient
            new_second = beta_two * m2[rows] + (1.0 - beta_two) * gradient * gradient
            nf_ref[rows] = new_first
            ns_ref[rows] = new_second
            weights = block(wf, y, (j * rsub, rsub))[...].astype(F32)
            update = new_first / (jnp.sqrt(new_second) + adam_eps)
            inner = weights - learn_rate * (update + decay_rate * weights)
            blend = blend_keep * inner + (1.0 - blend_keep) * full_anchor[j * rsub : (j + 1) * rsub]
            nw_ref[rows] = blend.astype(BF16)

    send_mid.start()
    send_c.start()
    ag_forward(0)
    send_x[0].start()
    send_x[1].start()
    transpose_weight()
    pl.when(late)(start_replica)
    mid_forward(0)
    ag_forward(1)
    pl.when(first)(start_replica)
    mid_forward(1)
    pl.when(early)(start_replica)
    ag_forward(2)
    make_part(0)
    rs_step(0)
    pl.when(not_early)(sum_z)
    send_x[2].start()
    ag_forward(3)
    make_part(1)
    send_x[3].start()
    rs_step(1)
    pl.when(early)(sum_z)
    send_x[4].start()
    pl.when(not_early)(outer)
    mid_forward(2)
    ag_forward(4)
    make_ig_partner()
    make_part(2)
    rs_step(2)
    pl.when(early)(outer)
    mid_forward(3)
    make_part(3)
    rs_step(3)
    share_core()
    mid_forward(4)
    make_ig_own()
    for copy in (send_mid, send_c, *send_x, *z1, *g2, swap):
        copy.wait_send()
    for s in range(NY // 2):
        for d in range(2):
            if s < 2:
                mid(d, s).wait_send()
            elif s == 2:
                pl.when(odd == d)(mid(d, 2).wait_send)
            for j in ag_subs(d, s):
                ag(d, s, j).wait_send()
            for j in range(RS_SUBS if s < NY // 2 - 1 else 0):
                rs(d, s, j).wait_send()
    finish()
    for copy in send_ig:
        copy.wait_recv()
    for copy in (*send_ig, *z4, g5):
        copy.wait_send()
    for d in range(2):
        for j in range(RS_SUBS):
            rs(d, NY // 2 - 1, j).wait_send()


def write_kernel(half_ref, ig_own, ig_recv, ig_mid, nw, nf, ns, na, nm, o_ig, o_nw, o_nf, o_ns, o_na, o_nm, sem):
    half = half_ref[0]
    copies = []
    for i in range(NPAIR):
        for which, source, start, size in (
            (half, ig_own.at[i], 0, PAIR),
            (1 - half, ig_recv.at[i, :, pl.ds(0, SIDE // 2)], 0, SIDE // 2),
            (1 - half, ig_mid.at[i], SIDE // 2, MID),
            (1 - half, ig_recv.at[i, :, pl.ds(SIDE // 2, SIDE // 2)], SIDE // 2 + MID, SIDE // 2),
        ):
            columns = pl.ds(pl.multiple_of(which * (D // 2) + i * PAIR + start, 128), size)
            copies.append((source, o_ig.at[:, columns]))
    copies += [(nw, o_nw), (nf, o_nf), (ns, o_ns), (na, o_na), (nm, o_nm)]
    copies = [pltpu.make_async_copy(src, dst, sem.at[k]) for k, (src, dst) in enumerate(copies)]
    for copy in copies:
        copy.start()
    for copy in copies:
        copy.wait()


def body(layer_input, cotangent, local_weight, first_moment, second_moment, anchor, outer_momentum):
    vmem = pl.BlockSpec(memory_space=pltpu.VMEM)
    hbm = pl.BlockSpec(memory_space=pl.ANY)
    shape = jax.ShapeDtypeStruct
    dma = pltpu.SemaphoreType.DMA
    small = shape((SHARE, ROWS), F32)
    wide = shape((ROWS, KV), F32)
    results = pl.pallas_call(
        step_kernel,
        out_shape=(
            shape((NPAIR, TOK, PAIR), BF16), shape((NPAIR, TOK, SIDE), BF16), shape((NPAIR, TOK, MID), BF16),
            shape((ROWS, KV), BF16), wide, wide, small, small,
        ),
        in_specs=[hbm] * 7,
        out_specs=[vmem] * 8,
        scratch_shapes=[
            pltpu.VMEM((NPAIR, TOK, PAIR), BF16),
            pltpu.VMEM((NPAIR, TOK, PAIR), BF16),
            pltpu.VMEM((TOK, KV), BF16),
            pltpu.VMEM((TOK, KV), BF16),
            pltpu.VMEM((NPAIR, PAIR, KV), BF16),
            pltpu.VMEM((NPAIR, MID, KV), BF16),
            pltpu.VMEM((NPAIR, PAIR, KV), F32),
            pltpu.VMEM((2, ROWS, KV // 2), BF16),
            pltpu.VMEM((2, 3, ROWS, KV), BF16),
            pltpu.VMEM((2, ROWS, KV // 2), BF16),
            pltpu.VMEM((2, 3, ROWS, KV), BF16),
            pltpu.VMEM((NPAIR, TOK, SIDE), BF16),
            pltpu.VMEM((TOK, MID), BF16),
            pltpu.VMEM((NZ, 2 * SHARE, 2 * ROWS), BF16),
            pltpu.VMEM((NZ - 1, 2 * SHARE, 2 * ROWS), BF16),
            pltpu.VMEM((2, SHARE, 2 * ROWS), F32),
            pltpu.VMEM((3, SHARE, 2 * ROWS), F32),
            pltpu.VMEM((2, SHARE, ROWS), F32),
            pltpu.VMEM((2, SHARE, ROWS), F32),
            pltpu.VMEM((NZ, 2, SHARE, 2 * ROWS), F32),
            pltpu.VMEM((ROWS, KV), F32),
            pltpu.VMEM((ROWS, KV), F32),
            dma((2 + NPAIR + 4,)),
            dma((4 + 2 * NPAIR,)), dma((4 + 2 * NPAIR,)),
            dma((2, NY // 2, AG_SUBS)), dma((2, NY // 2, AG_SUBS)),
            dma((2, 3)), dma((2, 3)),
            dma((2, NY // 2, RS_SUBS)), dma((2, NY // 2, RS_SUBS)),
            dma((NZ - 1,)), dma((NZ - 1,)),
            dma((NZ - 1,)), dma((NZ - 1,)),
            dma((5,)), dma((5,)),
            pltpu.SemaphoreType.REGULAR, pltpu.SemaphoreType.REGULAR,
        ],
        compiler_params=pltpu.CompilerParams(
            collective_id=0, has_side_effects=True, vmem_limit_bytes=40 << 20
        ),
        cost_estimate=pl.CostEstimate(flops=1_600_000_000, bytes_accessed=5_000_000, transcendentals=200_000),
        name="step",
    )(
        *(
            pltpu.with_memory_space_constraint(array, pltpu.HBM)
            for array in (
                layer_input, cotangent, local_weight[0], first_moment[0], second_moment[0], anchor.T, outer_momentum.T
            )
        )
    )
    half = (lax.axis_index("fsdp") // NY).astype(jnp.int32).reshape(1)
    outs = pl.pallas_call(
        write_kernel,
        out_shape=(shape((TOK, D), BF16), shape((ROWS, KV), BF16), wide, wide, small, small),
        in_specs=[pl.BlockSpec(memory_space=pltpu.SMEM)] + [vmem] * 8,
        out_specs=[hbm] * 6,
        scratch_shapes=[dma((4 * NPAIR + 5,))],
        name="write",
    )(half, *(pltpu.with_memory_space_constraint(array, pltpu.VMEM) for array in results))
    input_grad, new_weight, new_first, new_second, new_anchor, new_momentum = outs
    return input_grad, new_weight[None], new_first[None], new_second[None], new_anchor.T, new_momentum.T


def solution(mesh):
    in_specs = (
        P(("replica", "fsdp"), None),
        P(("replica", "fsdp"), None),
        P("replica", "fsdp", None),
        P("replica", "fsdp", None),
        P("replica", "fsdp", None),
        P("fsdp", "replica"),
        P("fsdp", "replica"),
    )
    out_specs = (
        P(("replica", "fsdp"), None),
        P("replica", "fsdp", None),
        P("replica", "fsdp", None),
        P("replica", "fsdp", None),
        P("fsdp", "replica"),
        P("fsdp", "replica"),
    )
    return jax.shard_map(body, mesh=mesh, in_specs=in_specs, out_specs=out_specs, check_vma=False)
```
